128 devices in a mesh: ctx: 32 (over y, x_hi, z), tp: 4 (over x_lo, core).
Axes of the slice: x: 4 (x_hi: 2, x_lo: 2; x = x_hi * 2 + x_lo), y: 4, z: 4, core: 2. Of those that a mesh axis runs over, the one named last changes fastest.
Arguments:
- prefill_queries: bfloat16 [6144, 8192], P('ctx', 'tp'), may hold values from -440 to 440, as said below
- prefill_key_values: bfloat16 [2, 6144, 1024], P(None, 'ctx', 'tp'), may hold values from -6 to 6
- fill_doc: int32 [6144], P('ctx'), may hold values from 0 to 3, never falling along the last dimension, each value on 1 to 3072 neighbouring positions
- decode_queries: bfloat16 [4, 32, 8192], P(None, None, 'tp'), may hold values from -440 to 440, as said below
- step_key_values: bfloat16 [4, 2, 32, 1024], P(None, None, None, 'tp'), may hold values from -6 to 6
- stored_key_values: bfloat16 [2, 32, 4096, 1024], P(None, None, 'ctx', 'tp'), may hold values from -6 to 6
- cached_len: int32 [32], replicated, may hold values from 1 to 4096, as said below
Outputs:
- fill_out: bfloat16 [6144, 8192], P('ctx', 'tp')
- step_out: bfloat16 [4, 32, 8192], P(None, None, 'tp')
The draws below stay inside these ranges and needn't reach their ends.
Inputs may be any that keep to these rules, and one draw needn't show every extreme that they name: `prefill_queries`: queries of order one or larger. `decode_queries`: queries of order one or larger. `fill_doc`: document ids never fall; each document holds at most 3072 positions. `cached_len`: some sequence has all 4096 positions cached.
All inputs are finite; a program needn't handle non-finite values.
Results may differ from the reference program's by a relative error of at most 0.006.
Values may be sent and summed in bfloat16 or wider, within the bound.
No kernel may reach another device: no remote copies, remote signals or barrier semaphores. Data moves between devices by JAX's collectives and lax.ppermute only.
A program may use at most 192 MiB of HBM per device.

```python
import math
import jax
import jax.numpy as jnp
import numpy as np
from jax import lax

QUERY_HEADS = 64
KEY_VALUE_HEADS = 8
HEAD_DIM = 128
DECODE_SEQUENCES = 32
DECODE_STEPS = 4
PREFILL_LENGTH = 6144
CACHE_SLOTS = 4096


def draw_prefill_queries(key, part):
    key = jax.random.fold_in(key, 11)
    value_rows = jnp.clip(3.0 * jax.random.normal(key, (PREFILL_LENGTH, QUERY_HEADS * HEAD_DIM), jnp.float32), -8.0, 8.0)
    return value_rows.astype(jnp.bfloat16)


def draw_decode_queries(key, part):
    key = jax.random.fold_in(key, 17)
    value_rows = jnp.clip(3.0 * jax.random.normal(key, (DECODE_STEPS, DECODE_SEQUENCES, QUERY_HEADS * HEAD_DIM), jnp.float32), -8.0, 8.0)
    return value_rows.astype(jnp.bfloat16)


def draw_cached_len(key, part):
    key = jax.random.fold_in(key, 23)
    lengths = jax.random.randint(key, (DECODE_SEQUENCES,), 1, CACHE_SLOTS + 1)
    chosen = jax.random.randint(jax.random.fold_in(key, 1), (), 0, DECODE_SEQUENCES)
    return jnp.where(jnp.arange(DECODE_SEQUENCES) == chosen, CACHE_SLOTS, lengths).astype(jnp.int32)


def block_scale(own_key, shape, split, smallest, high):
    def one(axis_at, shards_of):
        heights = jax.random.uniform(jax.random.fold_in(jax.random.fold_in(own_key, 6), axis_at), (shards_of,), jnp.float32, smallest / len(split), high / len(split))
        return jnp.repeat(jnp.exp(heights), shape[axis_at] // shards_of).reshape((-1,) + (1,) * (len(shape) - axis_at - 1))

    gain = one(*split[0])
    for cut in split[1:]:
        gain = gain * one(*cut)
    return gain


def split_up(count, total, reach, slope):
    loads = [(1 << 20) // math.isqrt(rank ** slope) + 1 for rank in range(2, count + 1)]
    rest, counts = total - reach - (count - 1), [1] * (count - 1)
    while rest > 0:
        free = [i for i in range(count - 1) if counts[i] < reach]
        whole, left = sum([loads[i] for i in free]), rest
        for i in free:
            addition = min(reach - counts[i], max(1, left * loads[i] // whole), rest)
            counts[i] = counts[i] + addition
            rest = rest - addition
    return np.array([reach] + counts)


def ragged(stream_key, amount, total, limit, slope):
    if amount == 2:
        one = jax.random.randint(stream_key, (), max(1, total - limit), min(limit, total - 1) + 1)
        return jnp.stack([one, total - one])
    sizes = jnp.asarray(split_up(amount, total, limit, slope), jnp.int32)
    twos = (amount - 1) // 2
    giver, taker = sizes[1:1 + 2 * twos:2], sizes[2:2 + 2 * twos:2]
    room = jnp.minimum(giver - 1, limit - taker)
    shifted = jax.random.randint(jax.random.fold_in(stream_key, 1), (twos,), 0, 1 << 20) % (room + 1)
    sizes = sizes.at[1:1 + 2 * twos:2].set(giver - shifted).at[2:2 + 2 * twos:2].set(taker + shifted)
    return sizes[jax.random.permutation(jax.random.fold_in(stream_key, 2), amount)]


def gaussian(own_key, dims, width, limit, pieces=(), kind=jnp.bfloat16):
    array = width * jax.random.normal(own_key, dims, jnp.float32)
    if pieces:
        array = array * block_scale(own_key, dims, pieces, -0.22, 0.18)
    return jnp.clip(array, -limit, limit).astype(kind)


def setup_inputs(seed: int = 0) -> dict:
    key_list = jax.random.split(jax.random.key(seed), 8)
    return {
        "prefill_queries": draw_prefill_queries(jax.random.fold_in(key_list[7], 71), 0),
        "prefill_key_values": gaussian(key_list[1], (2, PREFILL_LENGTH, KEY_VALUE_HEADS * HEAD_DIM), 1.0, 6.0, ((1, 32), (2, 4))),
        "fill_doc": jnp.searchsorted(jnp.cumsum(ragged(key_list[2], 4, PREFILL_LENGTH, PREFILL_LENGTH // 2, 0)), jnp.arange(PREFILL_LENGTH), side="right").astype(jnp.int32),
        "decode_queries": draw_decode_queries(jax.random.fold_in(key_list[7], 71), 0),
        "step_key_values": gaussian(key_list[4], (DECODE_STEPS, 2, DECODE_SEQUENCES, KEY_VALUE_HEADS * HEAD_DIM), 1.0, 6.0, ((3, 4),)),
        "stored_key_values": gaussian(key_list[5], (2, DECODE_SEQUENCES, CACHE_SLOTS, KEY_VALUE_HEADS * HEAD_DIM), 1.0, 6.0, ((2, 32), (3, 4))),
        "cached_len": draw_cached_len(jax.random.fold_in(key_list[7], 71), 0),
    }


NEG = -1.0e30


def fill_head(item):
    single_query, key_rows, value_rows, visible, scale = item[0], item[1], item[2], item[3], item[4]
    scores = jnp.einsum("gqd,kd->gqk", single_query, key_rows) * scale
    scores = jnp.where(visible[None], scores, NEG)
    peak = jnp.max(scores, axis=-1, keepdims=True)
    weights = jnp.where(visible[None], jnp.exp(scores - peak), 0.0)
    total = jnp.sum(weights, axis=-1, keepdims=True)
    rounded = lax.optimization_barrier(weights.astype(jnp.bfloat16)).astype(jnp.float32)
    return jnp.einsum("gqk,kd->gqd", rounded, value_rows) / total


def reference(prefill_queries, prefill_key_values, fill_doc, decode_queries, step_key_values, stored_key_values, cached_len):
    scale = HEAD_DIM ** -0.5
    query_group = QUERY_HEADS // KEY_VALUE_HEADS
    query_rows = prefill_queries.astype(jnp.float32).reshape(PREFILL_LENGTH, KEY_VALUE_HEADS, query_group, HEAD_DIM).transpose(1, 2, 0, 3)
    key_rows = prefill_key_values[0].astype(jnp.float32).reshape(PREFILL_LENGTH, KEY_VALUE_HEADS, HEAD_DIM).transpose(1, 0, 2)
    value_rows = prefill_key_values[1].astype(jnp.float32).reshape(PREFILL_LENGTH, KEY_VALUE_HEADS, HEAD_DIM).transpose(1, 0, 2)
    places = jnp.arange(PREFILL_LENGTH, dtype=jnp.int32)
    visible = (fill_doc[:, None] == fill_doc[None, :]) & (places[None, :] <= places[:, None])
    heads = lax.map(lambda item: fill_head((item[0], item[1], item[2], visible, scale)), (query_rows, key_rows, value_rows))
    fill_out = heads.transpose(2, 0, 1, 3).reshape(PREFILL_LENGTH, QUERY_HEADS * HEAD_DIM).astype(jnp.bfloat16)

    stored_keys = stored_key_values[0].astype(jnp.float32).reshape(DECODE_SEQUENCES, CACHE_SLOTS, KEY_VALUE_HEADS, HEAD_DIM)
    stored_values = stored_key_values[1].astype(jnp.float32).reshape(DECODE_SEQUENCES, CACHE_SLOTS, KEY_VALUE_HEADS, HEAD_DIM)
    step_keys = step_key_values[:, 0].astype(jnp.float32).reshape(DECODE_STEPS, DECODE_SEQUENCES, KEY_VALUE_HEADS, HEAD_DIM)
    step_values = step_key_values[:, 1].astype(jnp.float32).reshape(DECODE_STEPS, DECODE_SEQUENCES, KEY_VALUE_HEADS, HEAD_DIM)
    live = jnp.arange(CACHE_SLOTS, dtype=jnp.int32)[None, :] < cached_len[:, None]
    results = []
    for decode_index in range(DECODE_STEPS):
        single_query = decode_queries[decode_index].astype(jnp.float32).reshape(DECODE_SEQUENCES, KEY_VALUE_HEADS, query_group, HEAD_DIM)
        cache_scores = jnp.einsum("shgd,schd->shgc", single_query, stored_keys) * scale
        cache_scores = jnp.where(live[:, None, None, :], cache_scores, NEG)
        fresh_scores = jnp.einsum("shgd,tshd->shgt", single_query, step_keys[: decode_index + 1]) * scale
        peak = jnp.maximum(jnp.max(cache_scores, axis=-1), jnp.max(fresh_scores, axis=-1))[..., None]
        cache_w = jnp.where(live[:, None, None, :], jnp.exp(cache_scores - peak), 0.0)
        fresh_w = jnp.exp(fresh_scores - peak)
        total = jnp.sum(cache_w, axis=-1) + jnp.sum(fresh_w, axis=-1)
        cache_r = lax.optimization_barrier(cache_w.astype(jnp.bfloat16)).astype(jnp.float32)
        fresh_r = lax.optimization_barrier(fresh_w.astype(jnp.bfloat16)).astype(jnp.float32)
        summed = jnp.einsum("shgc,schd->shgd", cache_r, stored_values)
        summed = summed + jnp.einsum("shgt,tshd->shgd", fresh_r, step_values[: decode_index + 1])
        results.append((summed / total[..., None]).reshape(DECODE_SEQUENCES, QUERY_HEADS * HEAD_DIM))
    step_out = jnp.stack(results).astype(jnp.bfloat16)
    return fill_out, step_out
```

```python
import functools

import jax
import jax.numpy as jnp
from jax import lax
from jax.experimental import pallas as pl
from jax.experimental.pallas import tpu as pltpu
from jax.sharding import Mesh
from jax.sharding import PartitionSpec as P

HEAD_DIM = 128
GROUP = 8
STEPS = 4
SEQS = 32
SLOTS = 128
ROWS = 192
KV_HEADS = 2
HEADS = KV_HEADS * GROUP
PER_SEQ = STEPS * HEADS
PACKED = PER_SEQ + 16
BLOCK = 2 * ROWS + 16
FUSED = 4
LANES = FUSED * ROWS
CHUNK = 256
STATE = HEAD_DIM + 16
HIDDEN = -1e30
FLOOR = -1e20
TO_LOG2 = HEAD_DIM**-0.5 * 1.4426950408889634
CTX = ("y", "xh", "z")
PLANE = ("xh", "z")

NT = (((1,), (1,)), ((), ()))
TN = (((0,), (0,)), ((), ()))


def dot(a, b, dims):
    return lax.dot_general(a, b, dims, preferred_element_type=jnp.float32)


def decode_kernel(len_ref, me_ref, q_ref, kv_ref, fresh_ref, out_ref, *, per_step):
    base = pl.program_id(0) * per_step
    me = me_ref[0]
    lane = lax.broadcasted_iota(jnp.int32, (STEPS * GROUP, SLOTS), 1)
    stat_lane = lax.broadcasted_iota(jnp.int32, (STEPS * GROUP, HEAD_DIM), 1)
    pick = (
        lax.broadcasted_iota(jnp.int32, (16, HEAD_DIM), 0)
        == lax.broadcasted_iota(jnp.int32, (16, HEAD_DIM), 1)
    ).astype(jnp.bfloat16)
    row_step = lax.broadcasted_iota(jnp.int32, (STEPS * GROUP, 16), 0) // GROUP
    fresh_step = lax.broadcasted_iota(jnp.int32, (STEPS * GROUP, 16), 1)
    fresh_mask = fresh_step <= row_step

    def one(i, with_fresh):
        seq = base + i
        stats = []
        for h in range(KV_HEADS):
            at = pl.ds(h * HEAD_DIM, HEAD_DIM)
            rows = pl.ds(h * STEPS * GROUP, STEPS * GROUP)
            q = q_ref[i, rows, :]
            s = dot(q, kv_ref[0, i, :, at], NT) * TO_LOG2
            s = jnp.where(lane < len_ref[seq] - me * SLOTS, s, HIDDEN)
            m = jnp.maximum(jnp.max(s, axis=1, keepdims=True), FLOOR)
            if with_fresh:
                f = dot(q, fresh_ref[0, :, at], NT) * TO_LOG2
                f = jnp.where(fresh_mask, f, HIDDEN)
                m = jnp.maximum(m, jnp.max(f, axis=1, keepdims=True))
            m_hi = m.astype(jnp.bfloat16).astype(jnp.float32)
            m_lo = (m - m_hi).astype(jnp.bfloat16).astype(jnp.float32)
            m = m_hi + m_lo
            p = jnp.exp2(s - m)
            total = jnp.sum(p, axis=1, keepdims=True)
            o = dot(p.astype(jnp.bfloat16), kv_ref[1, i, :, at], (((1,), (0,)), ((), ())))
            if with_fresh:
                pf = jnp.exp2(f - m)
                total = total + jnp.sum(pf, axis=1, keepdims=True)
                o = o + dot(pf.astype(jnp.bfloat16), fresh_ref[1, :, at], (((1,), (0,)), ((), ())))
            l_hi = total.astype(jnp.bfloat16).astype(jnp.float32)
            l_lo = total - l_hi
            out_ref[i, rows, :] = o.astype(jnp.bfloat16)
            st = jnp.where(
                stat_lane == 0, m_hi, jnp.where(stat_lane == 1, m_lo, jnp.where(stat_lane == 2, l_hi, l_lo))
            )
            stats.append(st.astype(jnp.bfloat16))
        stats = jnp.concatenate(stats + [jnp.zeros((HEAD_DIM - PER_SEQ, HEAD_DIM), jnp.bfloat16)], axis=0)
        out_ref[i, PER_SEQ:, :] = dot(pick, stats, NT).astype(jnp.bfloat16)

    for i in range(per_step):
        one(i, False)
    for i in range(per_step):

        @pl.when(base + i == me)
        def _():
            one(i, True)


def decode_partials(lens, me, queries, cache, fresh):
    per_step = 4
    return pl.pallas_call(
        functools.partial(decode_kernel, per_step=per_step),
        grid_spec=pltpu.PrefetchScalarGridSpec(
            num_scalar_prefetch=2,
            grid=(SEQS // per_step,),
            in_specs=[
                pl.BlockSpec((per_step, PER_SEQ, HEAD_DIM), lambda i, *_: (i, 0, 0)),
                pl.BlockSpec((2, per_step, SLOTS, KV_HEADS * HEAD_DIM), lambda i, *_: (0, i, 0, 0)),
                pl.BlockSpec((2, 16, KV_HEADS * HEAD_DIM), lambda i, *_: (0, 0, 0)),
            ],
            out_specs=pl.BlockSpec((per_step, PACKED, HEAD_DIM), lambda i, *_: (i, 0, 0)),
        ),
        out_shape=jax.ShapeDtypeStruct((SEQS, PACKED, HEAD_DIM), jnp.bfloat16),
        compiler_params=pltpu.CompilerParams(vmem_limit_bytes=32 * 1024 * 1024),
        cost_estimate=pl.CostEstimate(flops=70_000_000, bytes_accessed=5_500_000, transcendentals=262144),
        name="decode_partials",
    )(lens, me, queries, cache, fresh)


def join_kernel(in_ref, out_ref, coef):
    peaks, totals = [], []
    for i in range(SEQS):
        st = in_ref[i, PER_SEQ:, :].astype(jnp.float32)
        peaks.append(st[0:1] + st[1:2])
        totals.append(st[2:3] + st[3:4])
    top = functools.reduce(jnp.maximum, peaks)
    scales = [jnp.exp2(m - top) for m in peaks]
    total = functools.reduce(jnp.add, [a * b for a, b in zip(scales, totals)])
    coef[...] = jnp.zeros_like(coef)
    for i in range(SEQS):
        coef[i : i + 1, :] = scales[i] / total
    columns = jnp.transpose(coef[...])
    acc = jnp.zeros((PER_SEQ, HEAD_DIM), jnp.float32)
    for i in range(SEQS):
        acc = acc + in_ref[i, :PER_SEQ, :].astype(jnp.float32) * columns[:PER_SEQ, i : i + 1]
    out_ref[...] = acc.astype(jnp.bfloat16)


def join_shares(shares):
    return pl.pallas_call(
        join_kernel,
        out_shape=jax.ShapeDtypeStruct((PER_SEQ, HEAD_DIM), jnp.bfloat16),
        in_specs=[pl.BlockSpec(memory_space=pltpu.VMEM)],
        out_specs=pl.BlockSpec(memory_space=pltpu.VMEM),
        scratch_shapes=[pltpu.VMEM((HEAD_DIM, HEAD_DIM), jnp.float32)],
        cost_estimate=pl.CostEstimate(flops=1_000_000, bytes_accessed=700_000, transcendentals=4096),
        name="join_shares",
    )(shares)


def prefill_kernel(valid_ref, info_ref, q_ref, *refs, counts, first, last):
    n_in = len(counts)
    blocks = refs[:n_in]
    rest = refs[n_in:]
    if first:
        state_in, rest = None, rest
    else:
        state_in, rest = rest[0], rest[1:]
    out_ref, rest = rest[0], rest[1:]
    if last:
        state, rest = rest[0], rest[1:]
    else:
        state = out_ref.at[0]
    low_ref, flag_ref = rest
    step = pl.program_id(0)
    places = [(r, b) for r, n in enumerate(counts) for b in range(n)]

    @pl.when(step == 0)
    def _():
        doc = info_ref[0:1, :]
        for at, (r, b) in enumerate(places):
            t = blocks[r][b, 2 * ROWS :, :].astype(jnp.float32)[0:1, :].astype(jnp.int32)
            low = jnp.where(doc == 1, t[:, 0:1], jnp.where(doc == 2, t[:, 1:2], jnp.where(doc == 3, t[:, 2:3], 0)))
            low_ref[at, 0:1, :] = low
            lowest, highest = jnp.min(low), jnp.max(low)
            seen = (valid_ref[at] > 0) & (lowest < ROWS)
            flag_ref[at] = jnp.where(seen, jnp.where(highest == 0, 1, 2), 0)

    if first:
        state[0:HEAD_DIM, :] = jnp.zeros((HEAD_DIM, LANES), jnp.float32)
        state[HEAD_DIM : HEAD_DIM + 8, :] = jnp.full((8, LANES), FLOOR, jnp.float32)
        state[HEAD_DIM + 8 :, :] = jnp.zeros((8, LANES), jnp.float32)
    else:
        state[...] = state_in[0]
    queries = jnp.concatenate([q_ref[:, j * HEAD_DIM : (j + 1) * HEAD_DIM] for j in range(FUSED)], axis=0)

    def attend(at, r, b, masked, own):
        keys = blocks[r][b, 0:ROWS, :]
        values = blocks[r][b, ROWS : 2 * ROWS, :]
        for c in range(LANES // CHUNK):
            on = slice(c * CHUNK, (c + 1) * CHUNK)
            s = dot(keys, queries[on], NT)
            if masked:
                j = lax.broadcasted_iota(jnp.int32, (ROWS, CHUNK), 0)
                sees = j >= low_ref[at, 0:1, on]
                if own:
                    sees = sees & (j <= info_ref[1:2, on])
                s = jnp.where(sees, s, HIDDEN)
            old = state[HEAD_DIM : HEAD_DIM + 1, on]
            peak = jnp.maximum(old, jnp.max(s, axis=0, keepdims=True))
            factor = jnp.exp2((old - peak) * TO_LOG2)
            p = jnp.exp2((s - peak) * TO_LOG2)
            total = state[HEAD_DIM + 8 : HEAD_DIM + 9, on] * factor + jnp.sum(p, axis=0, keepdims=True)
            state[HEAD_DIM : HEAD_DIM + 1, on] = peak
            state[HEAD_DIM + 8 : HEAD_DIM + 9, on] = total
            state[0:HEAD_DIM, on] = state[0:HEAD_DIM, on] * factor + dot(values, p.astype(jnp.bfloat16), TN)

    for at, (r, b) in enumerate(places):
        if first and at == 0:
            attend(at, r, b, True, True)
            continue

        @pl.when(flag_ref[at] == 1)
        def _():
            attend(at, r, b, False, False)

        @pl.when(flag_ref[at] == 2)
        def _():
            attend(at, r, b, True, False)

    if last:
        out = state[0:HEAD_DIM, :] / state[HEAD_DIM + 8 : HEAD_DIM + 9, :]
        out = jnp.transpose(out).astype(jnp.bfloat16)
        for j in range(FUSED):
            out_ref[:, j * HEAD_DIM : (j + 1) * HEAD_DIM] = out[j * ROWS : (j + 1) * ROWS]


def prefill_part(valid, info, queries, blocks, state, last, name):
    first = state is None
    counts = [b.shape[0] for b in blocks]
    n = sum(counts)
    steps = HEADS // FUSED
    q_spec = pl.BlockSpec((ROWS, FUSED * HEAD_DIM), lambda i, *_: (0, i))
    state_spec = pl.BlockSpec((1, STATE, LANES), lambda i, *_: (i, 0, 0))
    per_kv = steps // KV_HEADS
    in_specs = [pl.BlockSpec((8, LANES), lambda i, *_: (0, 0)), q_spec]
    in_specs += [pl.BlockSpec((c, BLOCK, HEAD_DIM), lambda i, *_: (0, 0, i // per_kv)) for c in counts]
    operands = [valid, info, queries, *blocks]
    if not first:
        in_specs.append(state_spec)
        operands.append(state)
    scratch = []
    if last:
        out_shape = jax.ShapeDtypeStruct((ROWS, HEADS * HEAD_DIM), jnp.bfloat16)
        out_spec = q_spec
        scratch.append(pltpu.VMEM((STATE, LANES), jnp.float32))
    else:
        out_shape = jax.ShapeDtypeStruct((steps, STATE, LANES), jnp.float32)
        out_spec = state_spec
    scratch += [pltpu.VMEM((n, 8, LANES), jnp.int32), pltpu.SMEM((n,), jnp.int32)]
    return pl.pallas_call(
        functools.partial(prefill_kernel, counts=counts, first=first, last=last),
        grid_spec=pltpu.PrefetchScalarGridSpec(
            num_scalar_prefetch=1,
            grid=(steps,),
            in_specs=in_specs,
            out_specs=out_spec,
            scratch_shapes=scratch,
        ),
        out_shape=out_shape,
        compiler_params=pltpu.CompilerParams(vmem_limit_bytes=48 * 1024 * 1024),
        cost_estimate=pl.CostEstimate(
            flops=4 * n * ROWS * ROWS * HEADS * HEAD_DIM,
            bytes_accessed=n * BLOCK * 512 + 4_000_000,
            transcendentals=n * ROWS * ROWS * HEADS,
        ),
        name=name,
    )(*operands)


def local(prefill_queries, prefill_key_values, fill_doc, decode_queries, step_key_values, stored_key_values, cached_len):
    y = lax.axis_index("y")
    place = lax.axis_index(PLANE)
    me = lax.axis_index(CTX).astype(jnp.int32)

    starts = jnp.sum(fill_doc[None, :] < jnp.arange(1, 4, dtype=jnp.int32)[:, None], axis=1)
    starts = jnp.pad(starts.astype(jnp.bfloat16), (0, HEAD_DIM - 3))
    starts = jnp.pad(jnp.concatenate([starts, starts])[None], ((0, 15), (0, 0)))
    own = jnp.concatenate([prefill_key_values[0], prefill_key_values[1], starts], axis=0)[None]
    back1 = lax.ppermute(own, "y", [(i, i + 1) for i in range(3)])
    back2 = lax.ppermute(own, "y", [(i, i + 2) for i in range(2)])

    queries = decode_queries.reshape(STEPS, SEQS, KV_HEADS, GROUP, HEAD_DIM)
    queries = queries.transpose(1, 2, 0, 3, 4).reshape(SEQS, PER_SEQ, HEAD_DIM)
    fresh = lax.dynamic_index_in_dim(step_key_values, me, axis=2, keepdims=False)
    fresh = jnp.pad(fresh.transpose(1, 0, 2), ((0, 0), (0, 16 - STEPS), (0, 0)))
    shares = decode_partials(cached_len, me[None], queries, stored_key_values, fresh)

    got, flags = [], []
    for k in range(1, 8):
        bit = 1 << (k.bit_length() - 1)
        to_later = (place & bit) == 0
        other = jnp.where(to_later, own, back2)
        packed = jnp.concatenate([back1, other], axis=0)
        got.append(lax.ppermute(packed, PLANE, [(i, i ^ k) for i in range(8)]))
        from_earlier = (place & bit) != 0
        flags.append(jnp.stack([y >= 1, from_earlier | (y >= 2)]).astype(jnp.int32))

    shares = lax.all_to_all(shares, CTX, 0, 0)
    mine = join_shares(shares)
    spread = lax.all_to_all(jnp.broadcast_to(mine[None], (SEQS,) + mine.shape), CTX, 0, 0)
    step_out = spread.reshape(SEQS, KV_HEADS, STEPS, GROUP, HEAD_DIM).transpose(2, 0, 1, 3, 4)
    step_out = step_out.reshape(STEPS, SEQS, HEADS * HEAD_DIM)

    info = jnp.stack([fill_doc, jnp.arange(ROWS, dtype=jnp.int32)])
    info = jnp.pad(jnp.tile(info, (1, FUSED)), ((0, 6), (0, 0)))
    valid0 = jnp.stack([y >= 0, y >= 1, y >= 2]).astype(jnp.int32)
    state = prefill_part(valid0, info, prefill_queries, [own, back1, back2], None, False, "prefill_own")
    for at, (a, b) in enumerate(((0, 2), (2, 4), (4, 7))):
        state = prefill_part(
            jnp.concatenate(flags[a:b]), info, prefill_queries, got[a:b], state, b == 7, "prefill_%d" % at
        )
    return state, step_out


def solution(mesh):
    fine = Mesh(mesh.devices.reshape(4, 2, 4, 2, 2), ("y", "xh", "z", "xl", "c"))
    tp = ("xl", "c")
    placed = (
        P(CTX, tp),
        P(None, CTX, tp),
        P(CTX),
        P(None, None, tp),
        P(None, None, None, tp),
        P(None, None, CTX, tp),
        P(),
    )
    return jax.shard_map(
        local,
        mesh=fine,
        in_specs=placed,
        out_specs=(P(CTX, tp), P(None, None, tp)),
        check_vma=False,
    )
```

```python
import functools

import jax
import jax.numpy as jnp
from jax import lax
from jax.experimental import pallas as pl
from jax.experimental.pallas import tpu as pltpu
from jax.sharding import Mesh
from jax.sharding import PartitionSpec as P

HEAD_DIM = 128
GROUP = 8
STEPS = 4
SEQS = 32
SLOTS = 128
ROWS = 192
KV_HEADS = 2
HEADS = KV_HEADS * GROUP
PER_KV = STEPS * GROUP
PER_SEQ = STEPS * HEADS
PACKED = PER_SEQ + 16
FUSED = 4
LANES = FUSED * ROWS
STATE = HEAD_DIM + 16
HIDDEN = -1e30
FLOOR = -1e20
NOWHERE = -1000000
TO_LOG2 = HEAD_DIM**-0.5 * 1.4426950408889634
CTX = ("y", "xh", "z")
PLANE = ("xh", "z")

NT = (((1,), (1,)), ((), ()))
TN = (((0,), (0,)), ((), ()))
NN = (((1,), (0,)), ((), ()))


def dot(a, b, dims):
    return lax.dot_general(a, b, dims, preferred_element_type=jnp.float32)


def halves(value):
    high = value.astype(jnp.bfloat16).astype(jnp.float32)
    return high, (value - high).astype(jnp.bfloat16).astype(jnp.float32)


def decode_kernel(len_ref, me_ref, q_ref, kv_ref, step_ref, doc_ref, out_ref, *, per_step):
    base = pl.program_id(0) * per_step
    me = me_ref[0]
    lane = lax.broadcasted_iota(jnp.int32, (PER_SEQ, SLOTS), 1)
    tile_row = lax.broadcasted_iota(jnp.int32, (16, HEAD_DIM), 0)
    tile_lane = lax.broadcasted_iota(jnp.int32, (16, HEAD_DIM), 1)
    pick = ((tile_row == tile_lane) & (tile_row < 4)).astype(jnp.bfloat16)

    doc = doc_ref[...]
    counts = jnp.zeros((16, HEAD_DIM), jnp.float32)
    for d in range(1, 4):
        below = jnp.sum((doc < d).astype(jnp.float32), axis=1, keepdims=True)
        counts = jnp.where((tile_row == 4) & (tile_lane == d - 1), below, counts)

    def pack_stats(m_hi, m_lo, total):
        l_hi, l_lo = halves(total)
        at = lax.broadcasted_iota(jnp.int32, (total.shape[0], HEAD_DIM), 1)
        st = jnp.where(at == 0, m_hi, jnp.where(at == 1, m_lo, jnp.where(at == 2, l_hi, l_lo)))
        return dot(pick, st.astype(jnp.bfloat16), NT)

    def scores(i):
        return jnp.concatenate(
            [
                dot(
                    q_ref[i, h * PER_KV : (h + 1) * PER_KV, :],
                    kv_ref[0, i, :, h * HEAD_DIM : (h + 1) * HEAD_DIM],
                    NT,
                )
                for h in range(KV_HEADS)
            ],
            axis=0,
        )

    s = jnp.concatenate(
        [jnp.where(lane < len_ref[base + i] - me * SLOTS, scores(i) * TO_LOG2, HIDDEN) for i in range(per_step)],
        axis=0,
    )
    m_hi, m_lo = halves(jnp.maximum(jnp.max(s, axis=1, keepdims=True), FLOOR))
    p = jnp.exp2(s - (m_hi + m_lo))
    tile = pack_stats(m_hi, m_lo, jnp.sum(p, axis=1, keepdims=True))
    p = p.astype(jnp.bfloat16)
    for i in range(per_step):
        for h in range(KV_HEADS):
            r = i * PER_SEQ + h * PER_KV
            o = dot(p[r : r + PER_KV], kv_ref[1, i, :, h * HEAD_DIM : (h + 1) * HEAD_DIM], NN)
            out_ref[i, h * PER_KV : (h + 1) * PER_KV, :] = o.astype(jnp.bfloat16)
    for i in range(0, per_step, 2):
        pair = tile[:, i * PER_SEQ : (i + 2) * PER_SEQ]
        out_ref[i, PER_SEQ:, :] = (pair + counts).astype(jnp.bfloat16)
        swapped = jnp.concatenate([pair[:, PER_SEQ:], pair[:, :PER_SEQ]], axis=1)
        out_ref[i + 1, PER_SEQ:, :] = (swapped + counts).astype(jnp.bfloat16)

    for i in range(per_step):

        @pl.when(base + i == me)
        def _():
            row = lax.broadcasted_iota(jnp.int32, (16, KV_HEADS * HEAD_DIM), 0) == lax.rem(me, 16)

            def fresh(kind):
                rows = [
                    jnp.sum(jnp.where(row, step_ref[t, kind].astype(jnp.float32), 0.0), axis=0, keepdims=True)
                    for t in range(STEPS)
                ]
                rows.append(jnp.zeros((16 - STEPS, KV_HEADS * HEAD_DIM), jnp.float32))
                return jnp.concatenate(rows, axis=0).astype(jnp.bfloat16)

            keys, values = fresh(0), fresh(1)
            t = lax.rem(lax.broadcasted_iota(jnp.int32, (PER_SEQ, 16), 0), PER_KV) // GROUP
            sees = lax.broadcasted_iota(jnp.int32, (PER_SEQ, 16), 1) <= t
            s = jnp.where(lane < len_ref[me] - me * SLOTS, scores(i) * TO_LOG2, HIDDEN)
            f = jnp.concatenate(
                [
                    dot(q_ref[i, h * PER_KV : (h + 1) * PER_KV, :], keys[:, h * HEAD_DIM : (h + 1) * HEAD_DIM], NT)
                    for h in range(KV_HEADS)
                ],
                axis=0,
            )
            f = jnp.where(sees, f * TO_LOG2, HIDDEN)
            m_hi, m_lo = halves(
                jnp.maximum(jnp.max(s, axis=1, keepdims=True), jnp.max(f, axis=1, keepdims=True))
            )
            p = jnp.exp2(s - (m_hi + m_lo))
            pf = jnp.exp2(f - (m_hi + m_lo))
            total = jnp.sum(p, axis=1, keepdims=True) + jnp.sum(pf, axis=1, keepdims=True)
            stats = [jnp.broadcast_to(x, (PER_SEQ, 1)) for x in (m_hi, m_lo, total)]
            stats = [jnp.concatenate([x, jnp.zeros_like(x)], axis=0) for x in stats]
            out_ref[i, PER_SEQ:, :] = (pack_stats(*stats) + counts).astype(jnp.bfloat16)
            p, pf = p.astype(jnp.bfloat16), pf.astype(jnp.bfloat16)
            for h in range(KV_HEADS):
                on, at = slice(h * PER_KV, (h + 1) * PER_KV), slice(h * HEAD_DIM, (h + 1) * HEAD_DIM)
                o = dot(p[on], kv_ref[1, i, :, at], NN) + dot(pf[on], values[:, at], NN)
                out_ref[i, on, :] = o.astype(jnp.bfloat16)


def decode_partials(lens, me, queries, cache, fresh, doc):
    per_step = 16
    return pl.pallas_call(
        functools.partial(decode_kernel, per_step=per_step),
        grid_spec=pltpu.PrefetchScalarGridSpec(
            num_scalar_prefetch=2,
            grid=(SEQS // per_step,),
            in_specs=[
                pl.BlockSpec((per_step, PER_SEQ, HEAD_DIM), lambda i, *_: (i, 0, 0)),
                pl.BlockSpec((2, per_step, SLOTS, KV_HEADS * HEAD_DIM), lambda i, *_: (0, i, 0, 0)),
                pl.BlockSpec((STEPS, 2, 16, KV_HEADS * HEAD_DIM), lambda i, lens, me: (0, 0, me[0] // 16, 0)),
                pl.BlockSpec((1, ROWS), lambda i, *_: (0, 0)),
            ],
            out_specs=pl.BlockSpec((per_step, PACKED, HEAD_DIM), lambda i, *_: (i, 0, 0)),
        ),
        out_shape=jax.ShapeDtypeStruct((SEQS, PACKED, HEAD_DIM), jnp.bfloat16),
        compiler_params=pltpu.CompilerParams(vmem_limit_bytes=56 * 1024 * 1024),
        cost_estimate=pl.CostEstimate(flops=70_000_000, bytes_accessed=5_500_000, transcendentals=262144),
        name="decode_partials",
    )(lens, me, queries, cache, fresh, doc)


def join_kernel(in_ref, out_ref, starts_ref, coef):
    peaks, totals, starts = [], [], jnp.zeros((1, HEAD_DIM), jnp.float32)
    for i in range(SEQS):
        st = in_ref[i, PER_SEQ:, :].astype(jnp.float32)
        peaks.append(st[0:1] + st[1:2])
        totals.append(st[2:3] + st[3:4])
        starts = starts + st[4:5]
    starts_ref[...] = jnp.broadcast_to(starts, (8, HEAD_DIM))
    top = functools.reduce(jnp.maximum, peaks)
    scales = [jnp.exp2(m - top) for m in peaks]
    total = functools.reduce(jnp.add, [a * b for a, b in zip(scales, totals)])
    coef[...] = jnp.zeros_like(coef)
    for i in range(SEQS):
        coef[i : i + 1, :] = scales[i] / total
    columns = jnp.transpose(coef[...])
    acc = jnp.zeros((PER_SEQ, HEAD_DIM), jnp.float32)
    for i in range(SEQS):
        acc = acc + in_ref[i, :PER_SEQ, :].astype(jnp.float32) * columns[:PER_SEQ, i : i + 1]
    acc = acc.astype(jnp.bfloat16)
    for i in range(SEQS):
        out_ref[i] = acc


def join_shares(shares):
    return pl.pallas_call(
        join_kernel,
        out_shape=(
            jax.ShapeDtypeStruct((SEQS, PER_SEQ, HEAD_DIM), jnp.bfloat16),
            jax.ShapeDtypeStruct((8, HEAD_DIM), jnp.float32),
        ),
        in_specs=[pl.BlockSpec(memory_space=pltpu.VMEM)],
        out_specs=(pl.BlockSpec(memory_space=pltpu.VMEM), pl.BlockSpec(memory_space=pltpu.VMEM)),
        scratch_shapes=[pltpu.VMEM((HEAD_DIM, HEAD_DIM), jnp.float32)],
        cost_estimate=pl.CostEstimate(flops=1_000_000, bytes_accessed=1_200_000, transcendentals=4096),
        name="join_shares",
    )(shares)


def prefill_kernel(base_ref, info_ref, starts_ref, q_ref, *refs, counts, first, last):
    blocks, rest = refs[: len(counts)], refs[len(counts) :]
    state_in = None
    if not first:
        state_in, rest = rest[0], rest[1:]
    out_ref, keys_ref, values_ref, since_ref, flag_ref = rest
    step = pl.program_id(0)
    places = [(r, b) for r, n in enumerate(counts) for b in range(n)]
    n = len(places)

    @pl.when(step == 0)
    def _():
        doc, starts = info_ref[0:1, :], starts_ref[0:1, :].astype(jnp.int32)
        since = jnp.where(
            doc == 1, starts[:, 0:1], jnp.where(doc == 2, starts[:, 1:2], jnp.where(doc == 3, starts[:, 2:3], 0))
        )
        since_ref[0:1, :] = since
        lowest, highest = jnp.min(since), jnp.max(since)
        some, whole = lowest - base_ref[0] < ROWS, highest <= base_ref[0]
        for at in range(1, n):
            some = some | (lowest - base_ref[at] < ROWS)
            whole = whole & (highest <= base_ref[at])
        flag_ref[0] = jnp.where(some, jnp.where(whole, 1, 2), 0)

    @pl.when(lax.rem(step, HEADS // FUSED // KV_HEADS) == 0)
    def _():
        for at, (r, b) in enumerate(places):
            on = slice(at * ROWS, (at + 1) * ROWS)
            keys_ref[on, :] = blocks[r][0, b]
            values_ref[on, :] = blocks[r][1, b]

    def attend(masked):
        queries = jnp.concatenate([q_ref[:, j * HEAD_DIM : (j + 1) * HEAD_DIM] for j in range(FUSED)], axis=0)
        s = dot(keys_ref[...], queries, NT)
        if masked:
            row = lax.broadcasted_iota(jnp.int32, (ROWS, LANES), 0)
            parts = []
            for at in range(n):
                sees = row >= since_ref[0:1, :] - base_ref[at]
                if first and at == 0:
                    sees = sees & (row <= info_ref[1:2, :])
                parts.append(jnp.where(sees, s[at * ROWS : (at + 1) * ROWS], HIDDEN))
            s = jnp.concatenate(parts, axis=0)
        peak = jnp.max(s, axis=0, keepdims=True)
        if first:
            peak = jnp.maximum(peak, FLOOR)
        else:
            old = state_in[0, HEAD_DIM : HEAD_DIM + 1, :]
            peak = jnp.maximum(old, peak)
            factor = jnp.exp2((old - peak) * TO_LOG2)
        p = jnp.exp2((s - peak) * TO_LOG2)
        total = jnp.sum(p, axis=0, keepdims=True)
        summed = dot(values_ref[...], p.astype(jnp.bfloat16), TN)
        if not first:
            total = total + state_in[0, HEAD_DIM + 8 : HEAD_DIM + 9, :] * factor
            summed = summed + state_in[0, 0:HEAD_DIM, :] * factor
        finish(peak, total, summed)

    def finish(peak, total, summed):
        if last:
            out = jnp.transpose(summed / total).astype(jnp.bfloat16)
            for j in range(FUSED):
                out_ref[:, j * HEAD_DIM : (j + 1) * HEAD_DIM] = out[j * ROWS : (j + 1) * ROWS]
        else:
            out_ref[0, 0:HEAD_DIM, :] = summed
            out_ref[0, HEAD_DIM : HEAD_DIM + 8, :] = jnp.broadcast_to(peak, (8, LANES))
            out_ref[0, HEAD_DIM + 8 :, :] = jnp.broadcast_to(total, (8, LANES))

    if first:
        attend(True)
        return

    @pl.when(flag_ref[0] == 0)
    def _():
        finish(
            state_in[0, HEAD_DIM : HEAD_DIM + 1, :],
            state_in[0, HEAD_DIM + 8 : HEAD_DIM + 9, :],
            state_in[0, 0:HEAD_DIM, :],
        )

    @pl.when(flag_ref[0] == 1)
    def _():
        attend(False)

    @pl.when(flag_ref[0] == 2)
    def _():
        attend(True)


def prefill_part(bases, info, starts, queries, blocks, state, last, name):
    first = state is None
    counts = [b.shape[1] for b in blocks]
    n = sum(counts)
    steps = HEADS // FUSED
    per_kv = steps // KV_HEADS
    q_spec = pl.BlockSpec((ROWS, FUSED * HEAD_DIM), lambda i, *_: (0, i))
    state_spec = pl.BlockSpec((1, STATE, LANES), lambda i, *_: (i, 0, 0))
    in_specs = [
        pl.BlockSpec((8, LANES), lambda i, *_: (0, 0)),
        pl.BlockSpec((8, HEAD_DIM), lambda i, *_: (0, 0)),
        q_spec,
    ]
    in_specs += [pl.BlockSpec((2, c, ROWS, HEAD_DIM), lambda i, *_: (0, 0, 0, i // per_kv)) for c in counts]
    operands = [bases, info, starts, queries, *blocks]
    if not first:
        in_specs.append(state_spec)
        operands.append(state)
    if last:
        out_shape = jax.ShapeDtypeStruct((ROWS, HEADS * HEAD_DIM), jnp.bfloat16)
        out_spec = q_spec
    else:
        out_shape = jax.ShapeDtypeStruct((steps, STATE, LANES), jnp.float32)
        out_spec = state_spec
    return pl.pallas_call(
        functools.partial(prefill_kernel, counts=counts, first=first, last=last),
        grid_spec=pltpu.PrefetchScalarGridSpec(
            num_scalar_prefetch=1,
            grid=(steps,),
            in_specs=in_specs,
            out_specs=out_spec,
            scratch_shapes=[
                pltpu.VMEM((n * ROWS, HEAD_DIM), jnp.bfloat16),
                pltpu.VMEM((n * ROWS, HEAD_DIM), jnp.bfloat16),
                pltpu.VMEM((8, LANES), jnp.int32),
                pltpu.SMEM((1,), jnp.int32),
            ],
        ),
        out_shape=out_shape,
        compiler_params=pltpu.CompilerParams(vmem_limit_bytes=48 * 1024 * 1024),
        cost_estimate=pl.CostEstimate(
            flops=4 * n * ROWS * ROWS * HEADS * HEAD_DIM,
            bytes_accessed=n * ROWS * 1024 + 4_000_000,
            transcendentals=n * ROWS * ROWS * HEADS,
        ),
        name=name,
    )(*operands)


ORDER = (4, 1, 3, 5, 2, 6, 7)
CALLS = ((0, 2), (2, 4), (4, 7))


def local(prefill_queries, prefill_key_values, fill_doc, decode_queries, step_key_values, stored_key_values, cached_len):
    y = lax.axis_index("y").astype(jnp.int32)
    place = lax.axis_index(PLANE).astype(jnp.int32)
    me = y * 8 + place

    own = prefill_key_values[:, None]
    back1 = lax.ppermute(own, "y", [(i, i + 1) for i in range(3)])
    back2 = lax.ppermute(own, "y", [(i, i + 2) for i in range(2)])

    queries = decode_queries.reshape(STEPS, SEQS, KV_HEADS, GROUP, HEAD_DIM)
    queries = queries.transpose(1, 2, 0, 3, 4).reshape(SEQS, PER_SEQ, HEAD_DIM)
    shares = decode_partials(cached_len, me[None], queries, stored_key_values, step_key_values, fill_doc[None])

    packs = {}
    for bit in (1, 2, 4):
        other = jnp.where((place & bit) == 0, own, back2)
        packs[bit] = jnp.concatenate([back1, other], axis=1)
    shares, packs = lax.optimization_barrier((shares, packs))
    got, bases = [], []
    for k in ORDER:
        bit = 1 << (k.bit_length() - 1)
        got.append(lax.ppermute(packs[bit], PLANE, [(i, i ^ k) for i in range(8)]))
        from_row = jnp.where((place & bit) != 0, y, y - 2)
        for row in (y - 1, from_row):
            bases.append(jnp.where(row >= 0, (row * 8 + (place ^ k)) * ROWS, NOWHERE))
    bases = jnp.stack(bases)

    shares = lax.all_to_all(shares, CTX, 0, 0)
    spread, starts = join_shares(shares)
    spread = lax.all_to_all(spread, CTX, 0, 0)
    step_out = spread.reshape(SEQS, KV_HEADS, STEPS, GROUP, HEAD_DIM).transpose(2, 0, 1, 3, 4)
    step_out = step_out.reshape(STEPS, SEQS, HEADS * HEAD_DIM)

    info = jnp.stack([fill_doc, jnp.arange(ROWS, dtype=jnp.int32)])
    info = jnp.pad(jnp.tile(info, (1, FUSED)), ((0, 6), (0, 0)))
    rows = [jnp.where(y >= d, (me - 8 * d) * ROWS, NOWHERE) for d in range(3)]
    state = None
    for at, (a, b) in enumerate(CALLS):
        blocks, base = got[a:b], bases[2 * a : 2 * b]
        if at == 0:
            blocks, base = [own, back1, back2] + blocks, jnp.concatenate([jnp.stack(rows), base])
        state = prefill_part(base, info, starts, prefill_queries, blocks, state, b == 7, "prefill_%d" % at)
    return state, step_out


def solution(mesh):
    fine = Mesh(mesh.devices.reshape(4, 2, 4, 2, 2), ("y", "xh", "z", "xl", "c"))
    tp = ("xl", "c")
    placed = (
        P(CTX, tp),
        P(None, CTX, tp),
        P(CTX),
        P(None, None, tp),
        P(None, None, None, tp),
        P(None, None, CTX, tp),
        P(),
    )
    return jax.shard_map(
        local,
        mesh=fine,
        in_specs=placed,
        out_specs=(P(CTX, tp), P(None, None, tp)),
        check_vma=False,
    )
```

```python
import functools

import jax
import jax.numpy as jnp
from jax import lax
from jax.experimental import pallas as pl
from jax.experimental.pallas import tpu as pltpu
from jax.sharding import Mesh
from jax.sharding import PartitionSpec as P

HEAD_DIM = 128
GROUP = 8
STEPS = 4
SEQS = 32
SLOTS = 128
ROWS = 192
KV_HEADS = 2
HEADS = KV_HEADS * GROUP
PER_KV = STEPS * GROUP
PER_SEQ = STEPS * HEADS
PACKED = PER_SEQ + 16
FUSED = 8
LANES = FUSED * ROWS
BLOCK = 2 * ROWS + 16
STATE = HEAD_DIM + 16
HIDDEN = -1e30
FLOOR = -1e20
NOWHERE = -1000000
TOO_LARGE = 2.0**100
TO_LOG2 = HEAD_DIM**-0.5 * 1.4426950408889634
CTX = ("y", "xh", "z")
PLANE = ("xh", "z")

NT = (((1,), (1,)), ((), ()))
TN = (((0,), (0,)), ((), ()))
NN = (((1,), (0,)), ((), ()))


def dot(a, b, dims):
    return lax.dot_general(a, b, dims, preferred_element_type=jnp.float32)


def halves(value):
    high = value.astype(jnp.bfloat16).astype(jnp.float32)
    return high, (value - high).astype(jnp.bfloat16).astype(jnp.float32)


def decode_kernel(len_ref, me_ref, q_ref, kv_ref, step_ref, out_ref, *, per_step):
    base = pl.program_id(0) * per_step
    me = me_ref[0]
    lane = lax.broadcasted_iota(jnp.int32, (PER_SEQ, SLOTS), 1)
    tile_row = lax.broadcasted_iota(jnp.int32, (16, HEAD_DIM), 0)
    tile_lane = lax.broadcasted_iota(jnp.int32, (16, HEAD_DIM), 1)
    pick = ((tile_row == tile_lane) & (tile_row < 4)).astype(jnp.bfloat16)

    def pack_stats(m_hi, m_lo, total):
        l_hi, l_lo = halves(total)
        at = lax.broadcasted_iota(jnp.int32, (total.shape[0], HEAD_DIM), 1)
        st = jnp.where(at == 0, m_hi, jnp.where(at == 1, m_lo, jnp.where(at == 2, l_hi, l_lo)))
        return dot(pick, st.astype(jnp.bfloat16), NT)

    def scores(i):
        return jnp.concatenate(
            [
                dot(
                    q_ref[i, h * PER_KV : (h + 1) * PER_KV, :],
                    kv_ref[0, i, :, h * HEAD_DIM : (h + 1) * HEAD_DIM],
                    NT,
                )
                for h in range(KV_HEADS)
            ],
            axis=0,
        )

    s = jnp.concatenate(
        [jnp.where(lane < len_ref[base + i] - me * SLOTS, scores(i) * TO_LOG2, HIDDEN) for i in range(per_step)],
        axis=0,
    )
    m_hi, m_lo = halves(jnp.maximum(jnp.max(s, axis=1, keepdims=True), FLOOR))
    p = jnp.exp2(s - (m_hi + m_lo))
    tile = pack_stats(m_hi, m_lo, jnp.sum(p, axis=1, keepdims=True))
    p = p.astype(jnp.bfloat16)
    for i in range(per_step):
        for h in range(KV_HEADS):
            r = i * PER_SEQ + h * PER_KV
            o = dot(p[r : r + PER_KV], kv_ref[1, i, :, h * HEAD_DIM : (h + 1) * HEAD_DIM], NN)
            out_ref[i, h * PER_KV : (h + 1) * PER_KV, :] = o.astype(jnp.bfloat16)
    for i in range(0, per_step, 2):
        pair = tile[:, i * PER_SEQ : (i + 2) * PER_SEQ]
        out_ref[i, PER_SEQ:, :] = pair.astype(jnp.bfloat16)
        swapped = jnp.concatenate([pair[:, PER_SEQ:], pair[:, :PER_SEQ]], axis=1)
        out_ref[i + 1, PER_SEQ:, :] = swapped.astype(jnp.bfloat16)

    @pl.when((me >= base) & (me < base + per_step))
    def _():
        i = me - base
        row = lax.broadcasted_iota(jnp.int32, (16, KV_HEADS * HEAD_DIM), 0) == lax.rem(me, 16)

        def fresh(kind):
            rows = [
                jnp.sum(jnp.where(row, step_ref[t, kind].astype(jnp.float32), 0.0), axis=0, keepdims=True)
                for t in range(STEPS)
            ]
            rows.append(jnp.zeros((16 - STEPS, KV_HEADS * HEAD_DIM), jnp.float32))
            return jnp.concatenate(rows, axis=0).astype(jnp.bfloat16)

        keys, values = fresh(0), fresh(1)
        t = lax.rem(lax.broadcasted_iota(jnp.int32, (PER_SEQ, 16), 0), PER_KV) // GROUP
        sees = lax.broadcasted_iota(jnp.int32, (PER_SEQ, 16), 1) <= t
        s = jnp.where(lane < len_ref[me] - me * SLOTS, scores(i) * TO_LOG2, HIDDEN)
        f = jnp.concatenate(
            [
                dot(q_ref[i, h * PER_KV : (h + 1) * PER_KV, :], keys[:, h * HEAD_DIM : (h + 1) * HEAD_DIM], NT)
                for h in range(KV_HEADS)
            ],
            axis=0,
        )
        f = jnp.where(sees, f * TO_LOG2, HIDDEN)
        m_hi, m_lo = halves(
            jnp.maximum(jnp.max(s, axis=1, keepdims=True), jnp.max(f, axis=1, keepdims=True))
        )
        p = jnp.exp2(s - (m_hi + m_lo))
        pf = jnp.exp2(f - (m_hi + m_lo))
        total = jnp.sum(p, axis=1, keepdims=True) + jnp.sum(pf, axis=1, keepdims=True)
        stats = [jnp.broadcast_to(x, (PER_SEQ, 1)) for x in (m_hi, m_lo, total)]
        stats = [jnp.concatenate([x, jnp.zeros_like(x)], axis=0) for x in stats]
        out_ref[i, PER_SEQ:, :] = pack_stats(*stats).astype(jnp.bfloat16)
        p, pf = p.astype(jnp.bfloat16), pf.astype(jnp.bfloat16)
        for h in range(KV_HEADS):
            on, at = slice(h * PER_KV, (h + 1) * PER_KV), slice(h * HEAD_DIM, (h + 1) * HEAD_DIM)
            o = dot(p[on], kv_ref[1, i, :, at], NN) + dot(pf[on], values[:, at], NN)
            out_ref[i, on, :] = o.astype(jnp.bfloat16)


def decode_partials(lens, me, queries, cache, fresh):
    per_step = 16
    return pl.pallas_call(
        functools.partial(decode_kernel, per_step=per_step),
        grid_spec=pltpu.PrefetchScalarGridSpec(
            num_scalar_prefetch=2,
            grid=(SEQS // per_step,),
            in_specs=[
                pl.BlockSpec((per_step, PER_SEQ, HEAD_DIM), lambda i, *_: (i, 0, 0)),
                pl.BlockSpec((2, per_step, SLOTS, KV_HEADS * HEAD_DIM), lambda i, *_: (0, i, 0, 0)),
                pl.BlockSpec((STEPS, 2, 16, KV_HEADS * HEAD_DIM), lambda i, lens, me: (0, 0, me[0] // 16, 0)),
            ],
            out_specs=pl.BlockSpec((per_step, PACKED, HEAD_DIM), lambda i, *_: (i, 0, 0)),
        ),
        out_shape=jax.ShapeDtypeStruct((SEQS, PACKED, HEAD_DIM), jnp.bfloat16),
        compiler_params=pltpu.CompilerParams(vmem_limit_bytes=62 * 1024 * 1024),
        cost_estimate=pl.CostEstimate(flops=70_000_000, bytes_accessed=5_500_000, transcendentals=262144),
        name="decode_partials",
    )(lens, me, queries, cache, fresh)


def join_kernel(in_ref, out_ref, coef):
    peaks, totals = [], []
    for i in range(SEQS):
        st = in_ref[i, PER_SEQ:, :].astype(jnp.float32)
        peaks.append(st[0:1] + st[1:2])
        totals.append(st[2:3] + st[3:4])
    top = functools.reduce(jnp.maximum, peaks)
    scales = [jnp.exp2(m - top) for m in peaks]
    total = functools.reduce(jnp.add, [a * b for a, b in zip(scales, totals)])
    coef[...] = jnp.zeros_like(coef)
    for i in range(SEQS):
        coef[i : i + 1, :] = scales[i] / total
    columns = jnp.transpose(coef[...])
    acc = jnp.zeros((PER_SEQ, HEAD_DIM), jnp.float32)
    for i in range(SEQS):
        acc = acc + in_ref[i, :PER_SEQ, :].astype(jnp.float32) * columns[:PER_SEQ, i : i + 1]
    acc = acc.astype(jnp.bfloat16)
    for i in range(SEQS):
        out_ref[i] = acc


def join_shares(shares):
    return pl.pallas_call(
        join_kernel,
        out_shape=jax.ShapeDtypeStruct((SEQS, PER_SEQ, HEAD_DIM), jnp.bfloat16),
        in_specs=[pl.BlockSpec(memory_space=pltpu.VMEM)],
        out_specs=pl.BlockSpec(memory_space=pltpu.VMEM),
        scratch_shapes=[pltpu.VMEM((HEAD_DIM, HEAD_DIM), jnp.float32)],
        cost_estimate=pl.CostEstimate(flops=1_000_000, bytes_accessed=1_200_000, transcendentals=4096),
        name="join_shares",
    )(shares)


def block_kernel(doc_ref, kv_ref, out_ref):
    lane = lax.rem(lax.broadcasted_iota(jnp.int32, (16, KV_HEADS * HEAD_DIM), 1), HEAD_DIM)
    row = jnp.zeros((16, KV_HEADS * HEAD_DIM), jnp.float32)
    for d in range(1, 4):
        below = jnp.sum((doc_ref[...] < d).astype(jnp.float32), axis=1, keepdims=True)
        row = jnp.where(lane == d - 1, below, row)
    out_ref[0, 0 : 2 * ROWS, :] = kv_ref[...]
    out_ref[0, 2 * ROWS :, :] = row.astype(jnp.bfloat16)


def make_block(doc, key_values):
    vmem = pl.BlockSpec(memory_space=pltpu.VMEM)
    return pl.pallas_call(
        block_kernel,
        out_shape=jax.ShapeDtypeStruct((1, BLOCK, KV_HEADS * HEAD_DIM), jnp.bfloat16),
        in_specs=[vmem, vmem],
        out_specs=vmem,
        cost_estimate=pl.CostEstimate(flops=1000, bytes_accessed=400_000, transcendentals=0),
        name="make_block",
    )(doc, key_values)


def pair_valid(y, place, k):
    later = (place & (1 << (k.bit_length() - 1))) != 0
    return [y >= 1, later | (y >= 2)]


def prefill_kernel(at_ref, doc_ref, q_ref, *refs, moves, groups, first, last):
    blocks, rest = refs[: len(groups_of(moves, first))], refs[len(groups_of(moves, first)) :]
    state_in = None
    if not first:
        state_in, rest = rest[0], rest[1:]
    out_ref, rest = rest[0], rest[1:]
    if last:
        state, rest = rest[0], rest[1:]
    else:
        state = out_ref.at[0]
    keys_ref, values_ref, queries_ref, low_ref, flag_ref = rest
    step = pl.program_id(0)
    y, place = at_ref[0], at_ref[1]
    counts = groups_of(moves, first)
    places = [(r, b) for r, n in enumerate(counts) for b in range(n)]
    n = len(places)
    valid = [y >= d for d in range(3)] if first else []
    for k in moves:
        valid += pair_valid(y, place, k)

    @pl.when(step == 0)
    def _():
        doc = doc_ref[...]
        lows = []
        for at, (r, b) in enumerate(places):
            t = blocks[r][b, 2 * ROWS :, :].astype(jnp.float32)[0:1, :].astype(jnp.int32)
            low = jnp.where(doc == 1, t[:, 0:1], jnp.where(doc == 2, t[:, 1:2], jnp.where(doc == 3, t[:, 2:3], 0)))
            low = jnp.where(valid[at], low, ROWS)
            low_ref[at, 0:1, :] = jnp.concatenate([low] * FUSED, axis=1)
            lows.append(low)
        for g, (lo, hi) in enumerate(groups):
            some = jnp.min(functools.reduce(jnp.minimum, lows[lo:hi])) < ROWS
            whole = jnp.max(functools.reduce(jnp.maximum, lows[lo:hi])) == 0
            flag_ref[g] = jnp.where(some, jnp.where(whole, 1, 2), 0)

    @pl.when(lax.rem(step, max(HEADS // FUSED // KV_HEADS, 1)) == 0)
    def _():
        for at, (r, b) in enumerate(places):
            on = slice(at * ROWS, (at + 1) * ROWS)
            keys_ref[on, :] = blocks[r][b, 0:ROWS, :]
            values_ref[on, :] = blocks[r][b, ROWS : 2 * ROWS, :]

    for j in range(FUSED):
        queries_ref[j * ROWS : (j + 1) * ROWS, :] = q_ref[:, j * HEAD_DIM : (j + 1) * HEAD_DIM]

    def scores(lo, hi, masked):
        s = dot(keys_ref[lo * ROWS : hi * ROWS, :], queries_ref[...], NT)
        if not masked:
            return s
        row = lax.broadcasted_iota(jnp.int32, (ROWS, LANES), 0)
        parts = []
        for at in range(lo, hi):
            sees = row >= low_ref[at, 0:1, :]
            if first and at == 0:
                sees = sees & (row <= lax.rem(lax.broadcasted_iota(jnp.int32, (1, LANES), 1), ROWS))
            parts.append(jnp.where(sees, s[(at - lo) * ROWS : (at - lo + 1) * ROWS], HIDDEN))
        return jnp.concatenate(parts, axis=0)

    def weighted(lo, hi, p):
        return dot(values_ref[lo * ROWS : hi * ROWS, :], p.astype(jnp.bfloat16), TN)

    def put(peak, total, summed):
        state[0:HEAD_DIM, :] = summed
        state[HEAD_DIM : HEAD_DIM + 8, :] = jnp.broadcast_to(peak, (8, LANES))
        state[HEAD_DIM + 8 :, :] = jnp.broadcast_to(total, (8, LANES))

    if first:
        s = scores(0, 1, True)
        peak = jnp.max(s, axis=0, keepdims=True)
        p = jnp.exp2((s - peak) * TO_LOG2)
        put(peak, jnp.sum(p, axis=0, keepdims=True), weighted(0, 1, p))
    else:
        state[...] = state_in[0]

    def add(lo, hi, masked):
        about = state[HEAD_DIM : HEAD_DIM + 1, :] * TO_LOG2
        p = jnp.exp2(scores(lo, hi, masked) * TO_LOG2 - about)
        state[HEAD_DIM + 8 :, :] = state[HEAD_DIM + 8 :, :] + jnp.sum(p, axis=0, keepdims=True)
        state[0:HEAD_DIM, :] = state[0:HEAD_DIM, :] + weighted(lo, hi, p)

    for g, (lo, hi) in enumerate(groups):

        @pl.when(flag_ref[g] == 1)
        def _():
            add(lo, hi, False)

        @pl.when(flag_ref[g] == 2)
        def _():
            add(lo, hi, True)

    @pl.when(jnp.logical_not(jnp.max(state[HEAD_DIM + 8 : HEAD_DIM + 9, :]) < TOO_LARGE))
    def _():
        s = scores(0, n, True)
        peak = jnp.max(s, axis=0, keepdims=True)
        if not first:
            old = state_in[0, HEAD_DIM : HEAD_DIM + 1, :]
            peak = jnp.maximum(old, peak)
        p = jnp.exp2((s - peak) * TO_LOG2)
        total, summed = jnp.sum(p, axis=0, keepdims=True), weighted(0, n, p)
        if not first:
            factor = jnp.exp2((old - peak) * TO_LOG2)
            total = total + state_in[0, HEAD_DIM + 8 : HEAD_DIM + 9, :] * factor
            summed = summed + state_in[0, 0:HEAD_DIM, :] * factor
        put(peak, total, summed)

    if last:
        out = state[0:HEAD_DIM, :] / state[HEAD_DIM + 8 : HEAD_DIM + 9, :]
        out = jnp.transpose(out).astype(jnp.bfloat16)
        for j in range(FUSED):
            out_ref[:, j * HEAD_DIM : (j + 1) * HEAD_DIM] = out[j * ROWS : (j + 1) * ROWS]


def groups_of(moves, first):
    return ([1, 1, 1] if first else []) + [2] * len(moves)


def prefill_part(at, doc, queries, blocks, moves, groups, state, last, name):
    first = state is None
    counts = groups_of(moves, first)
    n = sum(counts)
    steps = HEADS // FUSED
    per_kv = steps // KV_HEADS
    q_spec = pl.BlockSpec((ROWS, FUSED * HEAD_DIM), lambda i, *_: (0, i))
    state_spec = pl.BlockSpec((1, STATE, LANES), lambda i, *_: (i, 0, 0))
    in_specs = [
        pl.BlockSpec((1, ROWS), lambda i, *_: (0, 0)),
        q_spec,
    ]
    in_specs += [pl.BlockSpec((c, BLOCK, HEAD_DIM), lambda i, *_: (0, 0, i // per_kv)) for c in counts]
    operands = [at, doc, queries, *blocks]
    scratch = []
    if not first:
        in_specs.append(state_spec)
        operands.append(state)
    if last:
        out_shape = jax.ShapeDtypeStruct((ROWS, HEADS * HEAD_DIM), jnp.bfloat16)
        out_spec = q_spec
        scratch.append(pltpu.VMEM((STATE, LANES), jnp.float32))
    else:
        out_shape = jax.ShapeDtypeStruct((steps, STATE, LANES), jnp.float32)
        out_spec = state_spec
    scratch += [
        pltpu.VMEM((n * ROWS, HEAD_DIM), jnp.bfloat16),
        pltpu.VMEM((n * ROWS, HEAD_DIM), jnp.bfloat16),
        pltpu.VMEM((LANES, HEAD_DIM), jnp.bfloat16),
        pltpu.VMEM((n, 8, LANES), jnp.int32),
        pltpu.SMEM((len(groups),), jnp.int32),
    ]
    return pl.pallas_call(
        functools.partial(prefill_kernel, moves=moves, groups=groups, first=first, last=last),
        grid_spec=pltpu.PrefetchScalarGridSpec(
            num_scalar_prefetch=1,
            grid=(steps,),
            in_specs=in_specs,
            out_specs=out_spec,
            scratch_shapes=scratch,
        ),
        out_shape=out_shape,
        compiler_params=pltpu.CompilerParams(vmem_limit_bytes=62 * 1024 * 1024),
        cost_estimate=pl.CostEstimate(flops=4 * n * ROWS * ROWS * HEADS * HEAD_DIM, bytes_accessed=4_000_000, transcendentals=0),
        name=name,
    )(*operands)


MOVES = (4, 1, 3, 5, 2, 6, 7)
CALLS = ((0, 3), (3, 7))
GROUPS = (((1, 5), (5, 9)), ((0, 4), (4, 8)))


def local(prefill_queries, prefill_key_values, fill_doc, decode_queries, step_key_values, stored_key_values, cached_len):
    y = lax.axis_index("y").astype(jnp.int32)
    place = lax.axis_index(PLANE).astype(jnp.int32)
    me = y * 8 + place

    own = make_block(fill_doc[None], prefill_key_values.reshape(2 * ROWS, KV_HEADS * HEAD_DIM))
    back1 = lax.ppermute(own, "y", [(i, i + 1) for i in range(3)])
    back2 = lax.ppermute(own, "y", [(i, i + 2) for i in range(2)])

    queries = decode_queries.reshape(STEPS, SEQS, KV_HEADS, GROUP, HEAD_DIM)
    queries = queries.transpose(1, 2, 0, 3, 4).reshape(SEQS, PER_SEQ, HEAD_DIM)
    shares = decode_partials(cached_len, me[None], queries, stored_key_values, step_key_values)

    packs = {}
    for bit in (1, 2, 4):
        other = jnp.where((place & bit) == 0, own, back2)
        packs[bit] = jnp.concatenate([back1, other], axis=0)
    packs, shares = lax.optimization_barrier((packs, shares))
    got = []
    for k in MOVES:
        if len(got) == CALLS[0][1]:
            packs, got = lax.optimization_barrier((packs, got))
        bit = 1 << (k.bit_length() - 1)
        got.append(lax.ppermute(packs[bit], PLANE, [(i, i ^ k) for i in range(8)]))

    at, doc = jnp.stack([y, place]), fill_doc[None]

    def part(call, state):
        a, b = CALLS[call]
        blocks = got[a:b] if state is not None else [own, back1, back2] + got[a:b]
        last = call == len(CALLS) - 1
        return prefill_part(
            at, doc, prefill_queries, blocks, MOVES[a:b], GROUPS[call], state, last, "prefill_%d" % call
        )

    shares = lax.all_to_all(shares, CTX, 0, 0)
    state = part(0, None)
    shares, state = lax.optimization_barrier((shares, state))
    spread = lax.all_to_all(join_shares(shares), CTX, 0, 0)
    fill_out = part(1, state)
    step_out = spread.reshape(SEQS, KV_HEADS, STEPS, GROUP, HEAD_DIM).transpose(2, 0, 1, 3, 4)
    return fill_out, step_out.reshape(STEPS, SEQS, HEADS * HEAD_DIM)


def solution(mesh):
    fine = Mesh(mesh.devices.reshape(4, 2, 4, 2, 2), ("y", "xh", "z", "xl", "c"))
    tp = ("xl", "c")
    placed = (
        P(CTX, tp),
        P(None, CTX, tp),
        P(CTX),
        P(None, None, tp),
        P(None, None, None, tp),
        P(None, None, CTX, tp),
        P(),
    )
    return jax.shard_map(
        local,
        mesh=fine,
        in_specs=placed,
        out_specs=(P(CTX, tp), P(None, None, tp)),
        check_vma=False,
    )
```

```python
import functools

import jax
import jax.numpy as jnp
from jax import lax
from jax.experimental import pallas as pl
from jax.experimental.pallas import tpu as pltpu
from jax.sharding import Mesh
from jax.sharding import PartitionSpec as P

HEAD_DIM = 128
GROUP = 8
STEPS = 4
SEQS = 32
SLOTS = 128
ROWS = 192
KV_HEADS = 2
HEADS = KV_HEADS * GROUP
PER_KV = STEPS * GROUP
PER_SEQ = STEPS * HEADS
PACKED = PER_SEQ + 16
FUSED = 8
LANES = FUSED * ROWS
BLOCK = 2 * ROWS + 16
STATE = HEAD_DIM + 16
HIDDEN = -1e30
FLOOR = -1e20
NOWHERE = -1000000
TOO_LARGE = 2.0**100
TO_LOG2 = HEAD_DIM**-0.5 * 1.4426950408889634
CTX = ("y", "xh", "z")
PLANE = ("xh", "z")

NT = (((1,), (1,)), ((), ()))
TN = (((0,), (0,)), ((), ()))
NN = (((1,), (0,)), ((), ()))


def dot(a, b, dims):
    return lax.dot_general(a, b, dims, preferred_element_type=jnp.float32)


def halves(value):
    high = value.astype(jnp.bfloat16).astype(jnp.float32)
    return high, (value - high).astype(jnp.bfloat16).astype(jnp.float32)


def decode_kernel(len_ref, me_ref, q_ref, kv_ref, step_ref, out_ref, *, per_step):
    base = pl.program_id(0) * per_step
    me = me_ref[0]
    lane = lax.broadcasted_iota(jnp.int32, (PER_SEQ, SLOTS), 1)
    tile_row = lax.broadcasted_iota(jnp.int32, (16, HEAD_DIM), 0)
    tile_lane = lax.broadcasted_iota(jnp.int32, (16, HEAD_DIM), 1)
    pick = ((tile_row == tile_lane) & (tile_row < 4)).astype(jnp.bfloat16)

    def pack_stats(m_hi, m_lo, total):
        l_hi, l_lo = halves(total)
        at = lax.broadcasted_iota(jnp.int32, (total.shape[0], HEAD_DIM), 1)
        st = jnp.where(at == 0, m_hi, jnp.where(at == 1, m_lo, jnp.where(at == 2, l_hi, l_lo)))
        return dot(pick, st.astype(jnp.bfloat16), NT)

    def scores(i):
        return jnp.concatenate(
            [
                dot(
                    q_ref[i, h * PER_KV : (h + 1) * PER_KV, :],
                    kv_ref[0, i, :, h * HEAD_DIM : (h + 1) * HEAD_DIM],
                    NT,
                )
                for h in range(KV_HEADS)
            ],
            axis=0,
        )

    s = jnp.concatenate(
        [jnp.where(lane < len_ref[base + i] - me * SLOTS, scores(i) * TO_LOG2, HIDDEN) for i in range(per_step)],
        axis=0,
    )
    m_hi, m_lo = halves(jnp.maximum(jnp.max(s, axis=1, keepdims=True), FLOOR))
    p = jnp.exp2(s - (m_hi + m_lo))
    tile = pack_stats(m_hi, m_lo, jnp.sum(p, axis=1, keepdims=True))
    p = p.astype(jnp.bfloat16)
    for i in range(per_step):
        for h in range(KV_HEADS):
            r = i * PER_SEQ + h * PER_KV
            o = dot(p[r : r + PER_KV], kv_ref[1, i, :, h * HEAD_DIM : (h + 1) * HEAD_DIM], NN)
            out_ref[i, h * PER_KV : (h + 1) * PER_KV, :] = o.astype(jnp.bfloat16)
    for i in range(0, per_step, 2):
        pair = tile[:, i * PER_SEQ : (i + 2) * PER_SEQ]
        out_ref[i, PER_SEQ:, :] = pair.astype(jnp.bfloat16)
        swapped = jnp.concatenate([pair[:, PER_SEQ:], pair[:, :PER_SEQ]], axis=1)
        out_ref[i + 1, PER_SEQ:, :] = swapped.astype(jnp.bfloat16)

    @pl.when((me >= base) & (me < base + per_step))
    def _():
        i = me - base
        row = lax.broadcasted_iota(jnp.int32, (16, KV_HEADS * HEAD_DIM), 0) == lax.rem(me, 16)

        def fresh(kind):
            rows = [
                jnp.sum(jnp.where(row, step_ref[t, kind].astype(jnp.float32), 0.0), axis=0, keepdims=True)
                for t in range(STEPS)
            ]
            rows.append(jnp.zeros((16 - STEPS, KV_HEADS * HEAD_DIM), jnp.float32))
            return jnp.concatenate(rows, axis=0).astype(jnp.bfloat16)

        keys, values = fresh(0), fresh(1)
        t = lax.rem(lax.broadcasted_iota(jnp.int32, (PER_SEQ, 16), 0), PER_KV) // GROUP
        sees = lax.broadcasted_iota(jnp.int32, (PER_SEQ, 16), 1) <= t
        s = jnp.where(lane < len_ref[me] - me * SLOTS, scores(i) * TO_LOG2, HIDDEN)
        f = jnp.concatenate(
            [
                dot(q_ref[i, h * PER_KV : (h + 1) * PER_KV, :], keys[:, h * HEAD_DIM : (h + 1) * HEAD_DIM], NT)
                for h in range(KV_HEADS)
            ],
            axis=0,
        )
        f = jnp.where(sees, f * TO_LOG2, HIDDEN)
        m_hi, m_lo = halves(
            jnp.maximum(jnp.max(s, axis=1, keepdims=True), jnp.max(f, axis=1, keepdims=True))
        )
        p = jnp.exp2(s - (m_hi + m_lo))
        pf = jnp.exp2(f - (m_hi + m_lo))
        total = jnp.sum(p, axis=1, keepdims=True) + jnp.sum(pf, axis=1, keepdims=True)
        stats = [jnp.broadcast_to(x, (PER_SEQ, 1)) for x in (m_hi, m_lo, total)]
        stats = [jnp.concatenate([x, jnp.zeros_like(x)], axis=0) for x in stats]
        out_ref[i, PER_SEQ:, :] = pack_stats(*stats).astype(jnp.bfloat16)
        p, pf = p.astype(jnp.bfloat16), pf.astype(jnp.bfloat16)
        for h in range(KV_HEADS):
            on, at = slice(h * PER_KV, (h + 1) * PER_KV), slice(h * HEAD_DIM, (h + 1) * HEAD_DIM)
            o = dot(p[on], kv_ref[1, i, :, at], NN) + dot(pf[on], values[:, at], NN)
            out_ref[i, on, :] = o.astype(jnp.bfloat16)


def decode_partials(lens, me, queries, cache, fresh):
    per_step = 16
    return pl.pallas_call(
        functools.partial(decode_kernel, per_step=per_step),
        grid_spec=pltpu.PrefetchScalarGridSpec(
            num_scalar_prefetch=2,
            grid=(SEQS // per_step,),
            in_specs=[
                pl.BlockSpec((per_step, PER_SEQ, HEAD_DIM), lambda i, *_: (i, 0, 0)),
                pl.BlockSpec((2, per_step, SLOTS, KV_HEADS * HEAD_DIM), lambda i, *_: (0, i, 0, 0)),
                pl.BlockSpec((STEPS, 2, 16, KV_HEADS * HEAD_DIM), lambda i, lens, me: (0, 0, me[0] // 16, 0)),
            ],
            out_specs=pl.BlockSpec((per_step, PACKED, HEAD_DIM), lambda i, *_: (i, 0, 0)),
        ),
        out_shape=jax.ShapeDtypeStruct((SEQS, PACKED, HEAD_DIM), jnp.bfloat16),
        compiler_params=pltpu.CompilerParams(vmem_limit_bytes=62 * 1024 * 1024),
        cost_estimate=pl.CostEstimate(flops=70_000_000, bytes_accessed=5_500_000, transcendentals=262144),
        name="decode_partials",
    )(lens, me, queries, cache, fresh)


def join_kernel(in_ref, out_ref, coef):
    peaks, totals = [], []
    for i in range(SEQS):
        st = in_ref[i, PER_SEQ:, :].astype(jnp.float32)
        peaks.append(st[0:1] + st[1:2])
        totals.append(st[2:3] + st[3:4])
    top = functools.reduce(jnp.maximum, peaks)
    scales = [jnp.exp2(m - top) for m in peaks]
    total = functools.reduce(jnp.add, [a * b for a, b in zip(scales, totals)])
    coef[...] = jnp.zeros_like(coef)
    for i in range(SEQS):
        coef[i : i + 1, :] = scales[i] / total
    columns = jnp.transpose(coef[...])
    acc = jnp.zeros((PER_SEQ, HEAD_DIM), jnp.float32)
    for i in range(SEQS):
        acc = acc + in_ref[i, :PER_SEQ, :].astype(jnp.float32) * columns[:PER_SEQ, i : i + 1]
    acc = acc.astype(jnp.bfloat16)
    for i in range(SEQS):
        out_ref[i] = acc


def join_shares(shares):
    return pl.pallas_call(
        join_kernel,
        out_shape=jax.ShapeDtypeStruct((SEQS, PER_SEQ, HEAD_DIM), jnp.bfloat16),
        in_specs=[pl.BlockSpec(memory_space=pltpu.VMEM)],
        out_specs=pl.BlockSpec(memory_space=pltpu.VMEM),
        scratch_shapes=[pltpu.VMEM((HEAD_DIM, HEAD_DIM), jnp.float32)],
        cost_estimate=pl.CostEstimate(flops=1_000_000, bytes_accessed=1_200_000, transcendentals=4096),
        name="join_shares",
    )(shares)


def block_kernel(doc_ref, kv_ref, out_ref):
    lane = lax.rem(lax.broadcasted_iota(jnp.int32, (16, KV_HEADS * HEAD_DIM), 1), HEAD_DIM)
    row = jnp.zeros((16, KV_HEADS * HEAD_DIM), jnp.float32)
    for d in range(1, 4):
        below = jnp.sum((doc_ref[...] < d).astype(jnp.float32), axis=1, keepdims=True)
        row = jnp.where(lane == d - 1, below, row)
    out_ref[0, 0 : 2 * ROWS, :] = kv_ref[...]
    out_ref[0, 2 * ROWS :, :] = row.astype(jnp.bfloat16)


def make_block(doc, key_values):
    vmem = pl.BlockSpec(memory_space=pltpu.VMEM)
    return pl.pallas_call(
        block_kernel,
        out_shape=jax.ShapeDtypeStruct((1, BLOCK, KV_HEADS * HEAD_DIM), jnp.bfloat16),
        in_specs=[vmem, vmem],
        out_specs=vmem,
        cost_estimate=pl.CostEstimate(flops=1000, bytes_accessed=400_000, transcendentals=0),
        name="make_block",
    )(doc, key_values)


def block_valid(y, xh, z, kind):
    across = (xh == 1) | (y >= 2)
    if kind == "own":
        return [y >= 0]
    if kind == "row":
        return [y >= 1] * 4
    if kind == "back":
        return [y >= 2]
    if kind == "across":
        return [across]
    bit = 1 << (kind.bit_length() - 1)
    return [((z & bit) != 0) | (y >= 2), across]


COUNT = {"own": 1, "row": 4, "back": 1, "across": 1, 1: 2, 2: 2, 3: 2}


def prefill_kernel(at_ref, doc_ref, q_ref, *refs, sources, groups, first, last):
    blocks, rest = refs[: len(sources)], refs[len(sources) :]
    state_in = None
    if not first:
        state_in, rest = rest[0], rest[1:]
    out_ref, rest = rest[0], rest[1:]
    if last:
        state, rest = rest[0], rest[1:]
    else:
        state = out_ref.at[0]
    keys_ref, values_ref, queries_ref, low_ref, flag_ref = rest
    step = pl.program_id(0)
    y, xh, z = at_ref[0], at_ref[1], at_ref[2]
    counts = [COUNT[source] for source in sources]
    places = [(r, b) for r, n in enumerate(counts) for b in range(n)]
    n = len(places)
    valid = []
    for source in sources:
        valid += block_valid(y, xh, z, source)

    @pl.when(step == 0)
    def _():
        doc = doc_ref[...]
        lows = []
        for at, (r, b) in enumerate(places):
            t = blocks[r][b, 2 * ROWS :, :].astype(jnp.float32)[0:1, :].astype(jnp.int32)
            low = jnp.where(doc == 1, t[:, 0:1], jnp.where(doc == 2, t[:, 1:2], jnp.where(doc == 3, t[:, 2:3], 0)))
            low = jnp.where(valid[at], low, ROWS)
            low_ref[at, 0:1, :] = jnp.concatenate([low] * FUSED, axis=1)
            lows.append(low)
        for g, (lo, hi) in enumerate(groups):
            some = jnp.min(functools.reduce(jnp.minimum, lows[lo:hi])) < ROWS
            whole = jnp.max(functools.reduce(jnp.maximum, lows[lo:hi])) == 0
            flag_ref[g] = jnp.where(some, jnp.where(whole, 1, 2), 0)

    @pl.when(lax.rem(step, max(HEADS // FUSED // KV_HEADS, 1)) == 0)
    def _():
        for at, (r, b) in enumerate(places):
            on = slice(at * ROWS, (at + 1) * ROWS)
            keys_ref[on, :] = blocks[r][b, 0:ROWS, :]
            values_ref[on, :] = blocks[r][b, ROWS : 2 * ROWS, :]

    for j in range(FUSED):
        queries_ref[j * ROWS : (j + 1) * ROWS, :] = q_ref[:, j * HEAD_DIM : (j + 1) * HEAD_DIM]

    def scores(lo, hi, masked):
        s = dot(keys_ref[lo * ROWS : hi * ROWS, :], queries_ref[...], NT)
        if not masked:
            return s
        row = lax.broadcasted_iota(jnp.int32, (ROWS, LANES), 0)
        parts = []
        for at in range(lo, hi):
            sees = row >= low_ref[at, 0:1, :]
            if first and at == 0:
                sees = sees & (row <= lax.rem(lax.broadcasted_iota(jnp.int32, (1, LANES), 1), ROWS))
            parts.append(jnp.where(sees, s[(at - lo) * ROWS : (at - lo + 1) * ROWS], HIDDEN))
        return jnp.concatenate(parts, axis=0)

    def weighted(lo, hi, p):
        return dot(values_ref[lo * ROWS : hi * ROWS, :], p.astype(jnp.bfloat16), TN)

    def put(peak, total, summed):
        state[0:HEAD_DIM, :] = summed
        state[HEAD_DIM : HEAD_DIM + 8, :] = jnp.broadcast_to(peak, (8, LANES))
        state[HEAD_DIM + 8 :, :] = jnp.broadcast_to(total, (8, LANES))

    if first:
        s = scores(0, 1, True)
        peak = jnp.max(s, axis=0, keepdims=True)
        p = jnp.exp2((s - peak) * TO_LOG2)
        put(peak, jnp.sum(p, axis=0, keepdims=True), weighted(0, 1, p))
    else:
        state[...] = state_in[0]

    def add(lo, hi, masked):
        about = state[HEAD_DIM : HEAD_DIM + 1, :] * TO_LOG2
        p = jnp.exp2(scores(lo, hi, masked) * TO_LOG2 - about)
        state[HEAD_DIM + 8 :, :] = state[HEAD_DIM + 8 :, :] + jnp.sum(p, axis=0, keepdims=True)
        state[0:HEAD_DIM, :] = state[0:HEAD_DIM, :] + weighted(lo, hi, p)

    for g, (lo, hi) in enumerate(groups):

        @pl.when(flag_ref[g] == 1)
        def _():
            add(lo, hi, False)

        @pl.when(flag_ref[g] == 2)
        def _():
            add(lo, hi, True)

    @pl.when(jnp.logical_not(jnp.max(state[HEAD_DIM + 8 : HEAD_DIM + 9, :]) < TOO_LARGE))
    def _():
        s = scores(0, n, True)
        peak = jnp.max(s, axis=0, keepdims=True)
        if not first:
            old = state_in[0, HEAD_DIM : HEAD_DIM + 1, :]
            peak = jnp.maximum(old, peak)
        p = jnp.exp2((s - peak) * TO_LOG2)
        total, summed = jnp.sum(p, axis=0, keepdims=True), weighted(0, n, p)
        if not first:
            factor = jnp.exp2((old - peak) * TO_LOG2)
            total = total + state_in[0, HEAD_DIM + 8 : HEAD_DIM + 9, :] * factor
            summed = summed + state_in[0, 0:HEAD_DIM, :] * factor
        put(peak, total, summed)

    if last:
        out = state[0:HEAD_DIM, :] / state[HEAD_DIM + 8 : HEAD_DIM + 9, :]
        out = jnp.transpose(out).astype(jnp.bfloat16)
        for j in range(FUSED):
            out_ref[:, j * HEAD_DIM : (j + 1) * HEAD_DIM] = out[j * ROWS : (j + 1) * ROWS]


def prefill_part(at, doc, queries, blocks, sources, groups, state, last, name):
    first = state is None
    counts = [COUNT[source] for source in sources]
    n = sum(counts)
    steps = HEADS // FUSED
    per_kv = steps // KV_HEADS
    q_spec = pl.BlockSpec((ROWS, FUSED * HEAD_DIM), lambda i, *_: (0, i))
    state_spec = pl.BlockSpec((1, STATE, LANES), lambda i, *_: (i, 0, 0))
    in_specs = [
        pl.BlockSpec((1, ROWS), lambda i, *_: (0, 0)),
        q_spec,
    ]
    in_specs += [pl.BlockSpec((c, BLOCK, HEAD_DIM), lambda i, *_: (0, 0, i // per_kv)) for c in counts]
    operands = [at, doc, queries, *blocks]
    scratch = []
    if not first:
        in_specs.append(state_spec)
        operands.append(state)
    if last:
        out_shape = jax.ShapeDtypeStruct((ROWS, HEADS * HEAD_DIM), jnp.bfloat16)
        out_spec = q_spec
        scratch.append(pltpu.VMEM((STATE, LANES), jnp.float32))
    else:
        out_shape = jax.ShapeDtypeStruct((steps, STATE, LANES), jnp.float32)
        out_spec = state_spec
    scratch += [
        pltpu.VMEM((n * ROWS, HEAD_DIM), jnp.bfloat16),
        pltpu.VMEM((n * ROWS, HEAD_DIM), jnp.bfloat16),
        pltpu.VMEM((LANES, HEAD_DIM), jnp.bfloat16),
        pltpu.VMEM((n, 8, LANES), jnp.int32),
        pltpu.SMEM((len(groups),), jnp.int32),
    ]
    return pl.pallas_call(
        functools.partial(prefill_kernel, sources=sources, groups=groups, first=first, last=last),
        grid_spec=pltpu.PrefetchScalarGridSpec(
            num_scalar_prefetch=1,
            grid=(steps,),
            in_specs=in_specs,
            out_specs=out_spec,
            scratch_shapes=scratch,
        ),
        out_shape=out_shape,
        compiler_params=pltpu.CompilerParams(vmem_limit_bytes=62 * 1024 * 1024),
        cost_estimate=pl.CostEstimate(flops=4 * n * ROWS * ROWS * HEADS * HEAD_DIM, bytes_accessed=4_000_000, transcendentals=0),
        name=name,
    )(*operands)


SIDE = (2, 1, 3)


def local(prefill_queries, prefill_key_values, fill_doc, decode_queries, step_key_values, stored_key_values, cached_len):
    y, xh, z = [lax.axis_index(axis).astype(jnp.int32) for axis in CTX]
    me = (y * 2 + xh) * 4 + z

    own = make_block(fill_doc[None], prefill_key_values.reshape(2 * ROWS, KV_HEADS * HEAD_DIM))
    back1 = lax.ppermute(own, "y", [(i, i + 1) for i in range(3)])
    back2 = lax.ppermute(own, "y", [(i, i + 2) for i in range(2)])
    row = lax.all_to_all(jnp.broadcast_to(back1, (4,) + back1.shape[1:]), "z", 0, 0)
    across = lax.ppermute(jnp.where(xh == 0, own, back2), "xh", [(0, 1), (1, 0)])

    queries = decode_queries.reshape(STEPS, SEQS, KV_HEADS, GROUP, HEAD_DIM)
    queries = queries.transpose(1, 2, 0, 3, 4).reshape(SEQS, PER_SEQ, HEAD_DIM)
    shares = decode_partials(cached_len, me[None], queries, stored_key_values, step_key_values)

    far_row = lax.ppermute(row, "xh", [(0, 1), (1, 0)])
    packs = {bit: jnp.concatenate([jnp.where((z & bit) == 0, own, back2), across], axis=0) for bit in (1, 2)}
    packs, shares = lax.optimization_barrier((packs, shares))
    side = {k: lax.ppermute(packs[min(k, 2)], "z", [(i, i ^ k) for i in range(4)]) for k in SIDE}

    at, doc = jnp.stack([y, xh, z]), fill_doc[None]

    shares = lax.all_to_all(shares, CTX, 0, 0)
    state = prefill_part(
        at,
        doc,
        prefill_queries,
        [own, row, back2, across],
        ("own", "row", "back", "across"),
        ((1, 5), (5, 7)),
        None,
        False,
        "prefill_first",
    )
    shares, state = lax.optimization_barrier((shares, state))
    spread = lax.all_to_all(join_shares(shares), CTX, 0, 0)
    fill_out = prefill_part(
        at,
        doc,
        prefill_queries,
        [far_row] + [side[k] for k in SIDE],
        ("row",) + SIDE,
        ((0, 4), (4, 7), (7, 10)),
        state,
        True,
        "prefill_last",
    )
    spread, fill_out = lax.optimization_barrier((spread, fill_out))
    step_out = spread.reshape(SEQS, KV_HEADS, STEPS, GROUP, HEAD_DIM).transpose(2, 0, 1, 3, 4)
    return fill_out, step_out.reshape(STEPS, SEQS, HEADS * HEAD_DIM)


def solution(mesh):
    fine = Mesh(mesh.devices.reshape(4, 2, 4, 2, 2), ("y", "xh", "z", "xl", "c"))
    tp = ("xl", "c")
    placed = (
        P(CTX, tp),
        P(None, CTX, tp),
        P(CTX),
        P(None, None, tp),
        P(None, None, None, tp),
        P(None, None, CTX, tp),
        P(),
    )
    return jax.shard_map(
        local,
        mesh=fine,
        in_specs=placed,
        out_specs=(P(CTX, tp), P(None, None, tp)),
        check_vma=False,
    )
```

```python
import functools

import jax
import jax.numpy as jnp
from jax import lax
from jax.experimental import pallas as pl
from jax.experimental.pallas import tpu as pltpu
from jax.sharding import Mesh
from jax.sharding import PartitionSpec as P

HEAD_DIM = 128
GROUP = 8
STEPS = 4
SEQS = 32
SLOTS = 128
ROWS = 192
KV_HEADS = 2
HEADS = KV_HEADS * GROUP
PER_KV = STEPS * GROUP
PER_SEQ = STEPS * HEADS
PACKED = PER_SEQ + 16
FUSED = 8
LANES = FUSED * ROWS
BLOCK = 2 * ROWS + 16
STATE = HEAD_DIM + 16
HIDDEN = -1e30
FLOOR = -1e20
NOWHERE = -1000000
TOO_LARGE = 2.0**100
TO_LOG2 = HEAD_DIM**-0.5 * 1.4426950408889634
CTX = ("y", "xh", "z")
PLANE = ("xh", "z")

NT = (((1,), (1,)), ((), ()))
TN = (((0,), (0,)), ((), ()))
NN = (((1,), (0,)), ((), ()))


def dot(a, b, dims):
    return lax.dot_general(a, b, dims, preferred_element_type=jnp.float32)


def halves(value):
    high = value.astype(jnp.bfloat16).astype(jnp.float32)
    return high, (value - high).astype(jnp.bfloat16).astype(jnp.float32)


def decode_kernel(len_ref, me_ref, q_ref, kv_ref, step_ref, out_ref, *, per_step):
    base = pl.program_id(0) * per_step
    me = me_ref[0]
    lane = lax.broadcasted_iota(jnp.int32, (PER_SEQ, SLOTS), 1)
    tile_row = lax.broadcasted_iota(jnp.int32, (16, HEAD_DIM), 0)
    tile_lane = lax.broadcasted_iota(jnp.int32, (16, HEAD_DIM), 1)
    pick = ((tile_row == tile_lane) & (tile_row < 4)).astype(jnp.bfloat16)
    row = lax.broadcasted_iota(jnp.int32, (PER_SEQ, HEAD_DIM), 0)
    second = lax.rem(row, HEADS) >= GROUP

    def queries_of(i):
        q = jnp.concatenate([q_ref[t, i] for t in range(STEPS)], axis=0)
        none = jnp.zeros_like(q)
        return jnp.concatenate([jnp.where(second, none, q), jnp.where(second, q, none)], axis=1)

    def scores(i):
        return jnp.where(
            lane < len_ref[base + i] - me * SLOTS, dot(queries_of(i), kv_ref[0, i], NT) * TO_LOG2, HIDDEN
        )

    def own_head(o):
        return jnp.where(second, o[:, HEAD_DIM:], o[:, :HEAD_DIM])

    def pack_stats(m_hi, m_lo, total):
        l_hi, l_lo = halves(total)
        at = lax.broadcasted_iota(jnp.int32, (total.shape[0], HEAD_DIM), 1)
        st = jnp.where(at == 0, m_hi, jnp.where(at == 1, m_lo, jnp.where(at == 2, l_hi, l_lo)))
        return dot(pick, st.astype(jnp.bfloat16), NT)

    s = jnp.concatenate([scores(i) for i in range(per_step)], axis=0)
    m_hi, m_lo = halves(jnp.maximum(jnp.max(s, axis=1, keepdims=True), FLOOR))
    p = jnp.exp2(s - (m_hi + m_lo))
    tile = pack_stats(m_hi, m_lo, jnp.sum(p, axis=1, keepdims=True))
    p = p.astype(jnp.bfloat16)
    for i in range(per_step):
        o = dot(p[i * PER_SEQ : (i + 1) * PER_SEQ], kv_ref[1, i], NN)
        out_ref[i, :PER_SEQ, :] = own_head(o).astype(jnp.bfloat16)
    for i in range(0, per_step, 2):
        pair = tile[:, i * PER_SEQ : (i + 2) * PER_SEQ]
        out_ref[i, PER_SEQ:, :] = pair.astype(jnp.bfloat16)
        swapped = jnp.concatenate([pair[:, PER_SEQ:], pair[:, :PER_SEQ]], axis=1)
        out_ref[i + 1, PER_SEQ:, :] = swapped.astype(jnp.bfloat16)

    @pl.when((me >= base) & (me < base + per_step))
    def _():
        i = me - base
        chosen = lax.broadcasted_iota(jnp.int32, (16, KV_HEADS * HEAD_DIM), 0) == lax.rem(me, 16)

        def fresh(kind):
            rows = [
                jnp.sum(jnp.where(chosen, step_ref[t, kind].astype(jnp.float32), 0.0), axis=0, keepdims=True)
                for t in range(STEPS)
            ]
            rows.append(jnp.zeros((HEAD_DIM - STEPS, KV_HEADS * HEAD_DIM), jnp.float32))
            return jnp.concatenate(rows, axis=0).astype(jnp.bfloat16)

        s = scores(i)
        f = jnp.where(lane <= row // HEADS, dot(queries_of(i), fresh(0), NT) * TO_LOG2, HIDDEN)
        m_hi, m_lo = halves(jnp.maximum(jnp.max(s, axis=1, keepdims=True), jnp.max(f, axis=1, keepdims=True)))
        p = jnp.exp2(s - (m_hi + m_lo))
        pf = jnp.exp2(f - (m_hi + m_lo))
        total = jnp.sum(p, axis=1, keepdims=True) + jnp.sum(pf, axis=1, keepdims=True)
        stats = [jnp.concatenate([x, jnp.zeros_like(x)], axis=0) for x in (m_hi, m_lo, total)]
        out_ref[i, PER_SEQ:, :] = pack_stats(*stats).astype(jnp.bfloat16)
        o = dot(p.astype(jnp.bfloat16), kv_ref[1, i], NN) + dot(pf.astype(jnp.bfloat16), fresh(1), NN)
        out_ref[i, :PER_SEQ, :] = own_head(o).astype(jnp.bfloat16)


def decode_partials(lens, me, queries, cache, fresh):
    per_step = 16
    return pl.pallas_call(
        functools.partial(decode_kernel, per_step=per_step),
        grid_spec=pltpu.PrefetchScalarGridSpec(
            num_scalar_prefetch=2,
            grid=(SEQS // per_step,),
            in_specs=[
                pl.BlockSpec((STEPS, per_step, HEADS, HEAD_DIM), lambda i, *_: (0, i, 0, 0)),
                pl.BlockSpec((2, per_step, SLOTS, KV_HEADS * HEAD_DIM), lambda i, *_: (0, i, 0, 0)),
                pl.BlockSpec((STEPS, 2, 16, KV_HEADS * HEAD_DIM), lambda i, lens, me: (0, 0, me[0] // 16, 0)),
            ],
            out_specs=pl.BlockSpec((per_step, PACKED, HEAD_DIM), lambda i, *_: (i, 0, 0)),
        ),
        out_shape=jax.ShapeDtypeStruct((SEQS, PACKED, HEAD_DIM), jnp.bfloat16),
        compiler_params=pltpu.CompilerParams(vmem_limit_bytes=62 * 1024 * 1024),
        cost_estimate=pl.CostEstimate(flops=70_000_000, bytes_accessed=5_500_000, transcendentals=262144),
        name="decode_partials",
    )(lens, me, queries, cache, fresh)


def join_kernel(in_ref, out_ref, coef):
    peaks, totals = [], []
    for i in range(SEQS):
        st = in_ref[i, PER_SEQ:, :].astype(jnp.float32)
        peaks.append(st[0:1] + st[1:2])
        totals.append(st[2:3] + st[3:4])
    top = functools.reduce(jnp.maximum, peaks)
    scales = [jnp.exp2(m - top) for m in peaks]
    total = functools.reduce(jnp.add, [a * b for a, b in zip(scales, totals)])
    coef[...] = jnp.zeros_like(coef)
    for i in range(SEQS):
        coef[i : i + 1, :] = scales[i] / total
    columns = jnp.transpose(coef[...])
    acc = jnp.zeros((PER_SEQ, HEAD_DIM), jnp.float32)
    for i in range(SEQS):
        acc = acc + in_ref[i, :PER_SEQ, :].astype(jnp.float32) * columns[:PER_SEQ, i : i + 1]
    acc = acc.astype(jnp.bfloat16)
    for i in range(SEQS):
        out_ref[i] = acc


def join_shares(shares):
    return pl.pallas_call(
        join_kernel,
        out_shape=jax.ShapeDtypeStruct((SEQS, PER_SEQ, HEAD_DIM), jnp.bfloat16),
        in_specs=[pl.BlockSpec(memory_space=pltpu.VMEM)],
        out_specs=pl.BlockSpec(memory_space=pltpu.VMEM),
        scratch_shapes=[pltpu.VMEM((HEAD_DIM, HEAD_DIM), jnp.float32)],
        cost_estimate=pl.CostEstimate(flops=1_000_000, bytes_accessed=1_200_000, transcendentals=4096),
        name="join_shares",
    )(shares)


def block_kernel(doc_ref, kv_ref, out_ref):
    lane = lax.rem(lax.broadcasted_iota(jnp.int32, (16, KV_HEADS * HEAD_DIM), 1), HEAD_DIM)
    row = jnp.zeros((16, KV_HEADS * HEAD_DIM), jnp.float32)
    for d in range(1, 4):
        below = jnp.sum((doc_ref[...] < d).astype(jnp.float32), axis=1, keepdims=True)
        row = jnp.where(lane == d - 1, below, row)
    out_ref[0, 0 : 2 * ROWS, :] = kv_ref[...]
    out_ref[0, 2 * ROWS :, :] = row.astype(jnp.bfloat16)


def make_block(doc, key_values):
    vmem = pl.BlockSpec(memory_space=pltpu.VMEM)
    return pl.pallas_call(
        block_kernel,
        out_shape=jax.ShapeDtypeStruct((1, BLOCK, KV_HEADS * HEAD_DIM), jnp.bfloat16),
        in_specs=[vmem, vmem],
        out_specs=vmem,
        cost_estimate=pl.CostEstimate(flops=1000, bytes_accessed=400_000, transcendentals=0),
        name="make_block",
    )(doc, key_values)


def block_valid(y, xh, z, kind):
    across = (xh == 1) | (y >= 2)
    if kind == "own":
        return [y >= 0]
    if kind == "row":
        return [y >= 1] * 4
    if kind == "back":
        return [y >= 2]
    if kind == "across":
        return [across]
    bit = 1 << (kind.bit_length() - 1)
    return [((z & bit) != 0) | (y >= 2), across]


COUNT = {"own": 1, "row": 4, "back": 1, "across": 1, 1: 2, 2: 2, 3: 2}


def prefill_kernel(me_ref, doc_ref, q_ref, *refs, sources, order, groups, first, last):
    blocks, rest = refs[: len(sources)], refs[len(sources) :]
    state_in = None
    if not first:
        state_in, rest = rest[0], rest[1:]
    out_ref, rest = rest[0], rest[1:]
    if last:
        state, rest = rest[0], rest[1:]
    else:
        state = out_ref.at[0]
    keys_ref, values_ref, queries_ref, low_ref, flag_ref = rest
    step = pl.program_id(0)
    y, xh, z = me_ref[0] // 8, lax.rem(me_ref[0] // 4, 2), lax.rem(me_ref[0], 4)
    counts = [COUNT[source] for source in sources]
    places = [(r, b) for r, c in enumerate(counts) for b in range(c)]
    valid = []
    for source in sources:
        valid += block_valid(y, xh, z, source)
    places, valid = [places[i] for i in order], [valid[i] for i in order]
    n = len(places)

    @pl.when(step == 0)
    def _():
        doc = doc_ref[...]
        lows = []
        for at, (r, b) in enumerate(places):
            t = blocks[r][b, 2 * ROWS :, :].astype(jnp.float32)[0:1, :].astype(jnp.int32)
            low = jnp.where(doc == 1, t[:, 0:1], jnp.where(doc == 2, t[:, 1:2], jnp.where(doc == 3, t[:, 2:3], 0)))
            low = jnp.where(valid[at], low, ROWS)
            low_ref[at, 0:1, :] = jnp.concatenate([low] * FUSED, axis=1)
            lows.append(low)
        for g, (lo, hi) in enumerate(groups):
            some = jnp.min(functools.reduce(jnp.minimum, lows[lo:hi])) < ROWS
            inside = [jnp.where((low > 0) & (low < ROWS), 1, 0) for low in lows[lo:hi]]
            inside = jnp.max(functools.reduce(jnp.maximum, inside)) > 0
            flag_ref[g] = jnp.where(some, jnp.where(inside, 2, 1), 0)

    @pl.when(lax.rem(step, max(HEADS // FUSED // KV_HEADS, 1)) == 0)
    def _():
        for at, (r, b) in enumerate(places):
            on = slice(at * ROWS, (at + 1) * ROWS)
            keys_ref[on, :] = blocks[r][b, 0:ROWS, :]
            values_ref[on, :] = blocks[r][b, ROWS : 2 * ROWS, :]

    for j in range(FUSED):
        queries_ref[j * ROWS : (j + 1) * ROWS, :] = q_ref[:, j * HEAD_DIM : (j + 1) * HEAD_DIM]

    def scores(lo, hi, masked):
        s = dot(keys_ref[lo * ROWS : hi * ROWS, :], queries_ref[...], NT)
        if not masked:
            return s
        row = lax.broadcasted_iota(jnp.int32, (ROWS, LANES), 0)
        parts = []
        for at in range(lo, hi):
            sees = row >= low_ref[at, 0:1, :]
            if first and at == 0:
                sees = sees & (row <= lax.rem(lax.broadcasted_iota(jnp.int32, (1, LANES), 1), ROWS))
            parts.append(jnp.where(sees, s[(at - lo) * ROWS : (at - lo + 1) * ROWS], HIDDEN))
        return jnp.concatenate(parts, axis=0)

    def weighted(lo, hi, p):
        return dot(values_ref[lo * ROWS : hi * ROWS, :], p.astype(jnp.bfloat16), TN)

    def put(peak, total, summed):
        state[0:HEAD_DIM, :] = summed
        state[HEAD_DIM : HEAD_DIM + 8, :] = jnp.broadcast_to(peak, (8, LANES))
        state[HEAD_DIM + 8 :, :] = jnp.broadcast_to(total, (8, LANES))

    if first:
        s = scores(0, 1, True)
        peak = jnp.max(s, axis=0, keepdims=True)
        p = jnp.exp2((s - peak) * TO_LOG2)
        put(peak, jnp.sum(p, axis=0, keepdims=True), weighted(0, 1, p))
    else:
        state[...] = state_in[0]

    def add(lo, hi, masked):
        about = state[HEAD_DIM : HEAD_DIM + 1, :] * TO_LOG2
        s = scores(lo, hi, masked) * TO_LOG2
        if masked:
            s = s - about
        else:
            parts = []
            for at in range(lo, hi):
                part = s[(at - lo) * ROWS : (at - lo + 1) * ROWS]
                parts.append(part - jnp.where(low_ref[at, 0:1, :] < ROWS, about, -HIDDEN))
            s = jnp.concatenate(parts, axis=0)
        p = jnp.exp2(s)
        state[HEAD_DIM + 8 :, :] = state[HEAD_DIM + 8 :, :] + jnp.sum(p, axis=0, keepdims=True)
        state[0:HEAD_DIM, :] = state[0:HEAD_DIM, :] + weighted(lo, hi, p)

    for g, (lo, hi) in enumerate(groups):

        @pl.when(flag_ref[g] == 1)
        def _():
            add(lo, hi, False)

        @pl.when(flag_ref[g] == 2)
        def _():
            add(lo, hi, True)

    @pl.when(jnp.logical_not(jnp.max(state[HEAD_DIM + 8 : HEAD_DIM + 9, :]) < TOO_LARGE))
    def _():
        s = scores(0, n, True)
        peak = jnp.max(s, axis=0, keepdims=True)
        if not first:
            old = state_in[0, HEAD_DIM : HEAD_DIM + 1, :]
            peak = jnp.maximum(old, peak)
        p = jnp.exp2((s - peak) * TO_LOG2)
        total, summed = jnp.sum(p, axis=0, keepdims=True), weighted(0, n, p)
        if not first:
            factor = jnp.exp2((old - peak) * TO_LOG2)
            total = total + state_in[0, HEAD_DIM + 8 : HEAD_DIM + 9, :] * factor
            summed = summed + state_in[0, 0:HEAD_DIM, :] * factor
        put(peak, total, summed)

    if last:
        out = state[0:HEAD_DIM, :] / state[HEAD_DIM + 8 : HEAD_DIM + 9, :]
        out = jnp.transpose(out).astype(jnp.bfloat16)
        for j in range(FUSED):
            out_ref[:, j * HEAD_DIM : (j + 1) * HEAD_DIM] = out[j * ROWS : (j + 1) * ROWS]


def prefill_part(me, doc, queries, blocks, sources, order, groups, state, last, name):
    first = state is None
    counts = [COUNT[source] for source in sources]
    n = sum(counts)
    steps = HEADS // FUSED
    per_kv = steps // KV_HEADS
    q_spec = pl.BlockSpec((ROWS, FUSED * HEAD_DIM), lambda i, *_: (0, i))
    state_spec = pl.BlockSpec((1, STATE, LANES), lambda i, *_: (i, 0, 0))
    in_specs = [
        pl.BlockSpec((1, ROWS), lambda i, *_: (0, 0)),
        q_spec,
    ]
    in_specs += [pl.BlockSpec((c, BLOCK, HEAD_DIM), lambda i, *_: (0, 0, i // per_kv)) for c in counts]
    operands = [me, doc, queries, *blocks]
    scratch = []
    if not first:
        in_specs.append(state_spec)
        operands.append(state)
    if last:
        out_shape = jax.ShapeDtypeStruct((ROWS, HEADS * HEAD_DIM), jnp.bfloat16)
        out_spec = q_spec
        scratch.append(pltpu.VMEM((STATE, LANES), jnp.float32))
    else:
        out_shape = jax.ShapeDtypeStruct((steps, STATE, LANES), jnp.float32)
        out_spec = state_spec
    scratch += [
        pltpu.VMEM((n * ROWS, HEAD_DIM), jnp.bfloat16),
        pltpu.VMEM((n * ROWS, HEAD_DIM), jnp.bfloat16),
        pltpu.VMEM((LANES, HEAD_DIM), jnp.bfloat16),
        pltpu.VMEM((n, 8, LANES), jnp.int32),
        pltpu.SMEM((len(groups),), jnp.int32),
    ]
    return pl.pallas_call(
        functools.partial(prefill_kernel, sources=sources, order=order, groups=groups, first=first, last=last),
        grid_spec=pltpu.PrefetchScalarGridSpec(
            num_scalar_prefetch=1,
            grid=(steps,),
            in_specs=in_specs,
            out_specs=out_spec,
            scratch_shapes=scratch,
        ),
        out_shape=out_shape,
        compiler_params=pltpu.CompilerParams(vmem_limit_bytes=62 * 1024 * 1024),
        cost_estimate=pl.CostEstimate(flops=4 * n * ROWS * ROWS * HEADS * HEAD_DIM, bytes_accessed=4_000_000, transcendentals=0),
        name=name,
    )(*operands)


SIDE = (2, 1, 3)


def local(prefill_queries, prefill_key_values, fill_doc, decode_queries, step_key_values, stored_key_values, cached_len):
    y, xh, z = [lax.axis_index(axis).astype(jnp.int32) for axis in CTX]
    me = (y * 2 + xh) * 4 + z

    own = make_block(fill_doc[None], prefill_key_values.reshape(2 * ROWS, KV_HEADS * HEAD_DIM))
    back1 = lax.ppermute(own, "y", [(i, i + 1) for i in range(3)])
    back2 = lax.ppermute(own, "y", [(i, i + 2) for i in range(2)])
    row = lax.all_to_all(jnp.broadcast_to(back1, (4,) + back1.shape[1:]), "z", 0, 0)
    across = lax.ppermute(jnp.where(xh == 0, own, back2), "xh", [(0, 1), (1, 0)])

    queries = decode_queries.reshape(STEPS, SEQS, HEADS, HEAD_DIM)
    shares = decode_partials(cached_len, me[None], queries, stored_key_values, step_key_values)

    far_row = lax.ppermute(row, "xh", [(0, 1), (1, 0)])
    packs = {bit: jnp.concatenate([jnp.where((z & bit) == 0, own, back2), across], axis=0) for bit in (1, 2)}
    packs, shares = lax.optimization_barrier((packs, shares))
    side = {k: lax.ppermute(packs[min(k, 2)], "z", [(i, i ^ k) for i in range(4)]) for k in SIDE}

    doc = fill_doc[None]

    shares = lax.all_to_all(shares, CTX, 0, 0)
    state = prefill_part(
        me[None],
        doc,
        prefill_queries,
        [own, row, back2, across],
        ("own", "row", "back", "across"),
        tuple(range(7)),
        ((1, 5), (5, 7)),
        None,
        False,
        "prefill_first",
    )
    shares, state = lax.optimization_barrier((shares, state))
    spread = lax.all_to_all(join_shares(shares), CTX, 0, 0)
    fill_out = prefill_part(
        me[None],
        doc,
        prefill_queries,
        [far_row] + [side[k] for k in SIDE],
        ("row",) + SIDE,
        (0, 1, 2, 3, 5, 7, 9, 4, 6, 8),
        ((0, 4), (4, 7), (7, 10)),
        state,
        True,
        "prefill_last",
    )
    spread, fill_out = lax.optimization_barrier((spread, fill_out))
    step_out = spread.reshape(SEQS, STEPS, HEADS, HEAD_DIM).transpose(1, 0, 2, 3)
    return fill_out, step_out.reshape(STEPS, SEQS, HEADS * HEAD_DIM)


def solution(mesh):
    fine = Mesh(mesh.devices.reshape(4, 2, 4, 2, 2), ("y", "xh", "z", "xl", "c"))
    tp = ("xl", "c")
    placed = (
        P(CTX, tp),
        P(None, CTX, tp),
        P(CTX),
        P(None, None, tp),
        P(None, None, None, tp),
        P(None, None, CTX, tp),
        P(),
    )
    return jax.shard_map(
        local,
        mesh=fine,
        in_specs=placed,
        out_specs=(P(CTX, tp), P(None, None, tp)),
        check_vma=False,
    )
```

```python
import functools

import jax
import jax.numpy as jnp
from jax import lax
from jax.experimental import pallas as pl
from jax.experimental.pallas import tpu as pltpu
from jax.sharding import Mesh
from jax.sharding import PartitionSpec as P

HEAD_DIM = 128
GROUP = 8
STEPS = 4
SEQS = 32
SLOTS = 128
ROWS = 192
KV_HEADS = 2
HEADS = KV_HEADS * GROUP
PER_KV = STEPS * GROUP
PER_SEQ = STEPS * HEADS
PACKED = PER_SEQ + 16
FUSED = 8
LANES = FUSED * ROWS
BLOCK = 2 * ROWS + 16
STATE = HEAD_DIM + 16
HIDDEN = -1e30
FLOOR = -1e20
NOWHERE = -1000000
TOO_LARGE = 2.0**100
HIDDEN_KEY = 4
TO_LOG2 = HEAD_DIM**-0.5 * 1.4426950408889634
CTX = ("y", "xh", "z")
PLANE = ("xh", "z")

NT = (((1,), (1,)), ((), ()))
TN = (((0,), (0,)), ((), ()))
NN = (((1,), (0,)), ((), ()))


def dot(a, b, dims):
    return lax.dot_general(a, b, dims, preferred_element_type=jnp.float32)


def halves(value):
    high = value.astype(jnp.bfloat16).astype(jnp.float32)
    return high, (value - high).astype(jnp.bfloat16).astype(jnp.float32)


def decode_kernel(len_ref, me_ref, q_ref, kv_ref, step_ref, out_ref, *, per_step):
    base = pl.program_id(0) * per_step
    me = me_ref[0]
    lane = lax.broadcasted_iota(jnp.int32, (PER_SEQ, SLOTS), 1)
    tile_row = lax.broadcasted_iota(jnp.int32, (16, HEAD_DIM), 0)
    tile_lane = lax.broadcasted_iota(jnp.int32, (16, HEAD_DIM), 1)
    pick = ((tile_row == tile_lane) & (tile_row < 4)).astype(jnp.bfloat16)
    row = lax.broadcasted_iota(jnp.int32, (PER_SEQ, HEAD_DIM), 0)
    second = lax.rem(row, HEADS) >= GROUP

    def queries_of(i):
        q = jnp.concatenate([q_ref[t, i] for t in range(STEPS)], axis=0)
        none = jnp.zeros_like(q)
        return jnp.concatenate([jnp.where(second, none, q), jnp.where(second, q, none)], axis=1)

    def scores(i):
        return jnp.where(
            lane < len_ref[base + i] - me * SLOTS, dot(queries_of(i), kv_ref[0, i], NT) * TO_LOG2, HIDDEN
        )

    def own_head(o):
        return jnp.where(second, o[:, HEAD_DIM:], o[:, :HEAD_DIM])

    def pack_stats(m_hi, m_lo, total):
        l_hi, l_lo = halves(total)
        at = lax.broadcasted_iota(jnp.int32, (total.shape[0], HEAD_DIM), 1)
        st = jnp.where(at == 0, m_hi, jnp.where(at == 1, m_lo, jnp.where(at == 2, l_hi, l_lo)))
        return dot(pick, st.astype(jnp.bfloat16), NT)

    s = jnp.concatenate([scores(i) for i in range(per_step)], axis=0)
    m_hi, m_lo = halves(jnp.maximum(jnp.max(s, axis=1, keepdims=True), FLOOR))
    p = jnp.exp2(s - (m_hi + m_lo))
    tile = pack_stats(m_hi, m_lo, jnp.sum(p, axis=1, keepdims=True))
    p = p.astype(jnp.bfloat16)
    for i in range(per_step):
        o = dot(p[i * PER_SEQ : (i + 1) * PER_SEQ], kv_ref[1, i], NN)
        out_ref[i, :PER_SEQ, :] = own_head(o).astype(jnp.bfloat16)
    for i in range(0, per_step, 2):
        pair = tile[:, i * PER_SEQ : (i + 2) * PER_SEQ]
        out_ref[i, PER_SEQ:, :] = pair.astype(jnp.bfloat16)
        swapped = jnp.concatenate([pair[:, PER_SEQ:], pair[:, :PER_SEQ]], axis=1)
        out_ref[i + 1, PER_SEQ:, :] = swapped.astype(jnp.bfloat16)

    @pl.when((me >= base) & (me < base + per_step))
    def _():
        i = me - base
        chosen = lax.broadcasted_iota(jnp.int32, (16, KV_HEADS * HEAD_DIM), 0) == lax.rem(me, 16)

        def fresh(kind):
            rows = [
                jnp.sum(jnp.where(chosen, step_ref[t, kind].astype(jnp.float32), 0.0), axis=0, keepdims=True)
                for t in range(STEPS)
            ]
            rows.append(jnp.zeros((HEAD_DIM - STEPS, KV_HEADS * HEAD_DIM), jnp.float32))
            return jnp.concatenate(rows, axis=0).astype(jnp.bfloat16)

        s = scores(i)
        f = jnp.where(lane <= row // HEADS, dot(queries_of(i), fresh(0), NT) * TO_LOG2, HIDDEN)
        m_hi, m_lo = halves(jnp.maximum(jnp.max(s, axis=1, keepdims=True), jnp.max(f, axis=1, keepdims=True)))
        p = jnp.exp2(s - (m_hi + m_lo))
        pf = jnp.exp2(f - (m_hi + m_lo))
        total = jnp.sum(p, axis=1, keepdims=True) + jnp.sum(pf, axis=1, keepdims=True)
        stats = [jnp.concatenate([x, jnp.zeros_like(x)], axis=0) for x in (m_hi, m_lo, total)]
        out_ref[i, PER_SEQ:, :] = pack_stats(*stats).astype(jnp.bfloat16)
        o = dot(p.astype(jnp.bfloat16), kv_ref[1, i], NN) + dot(pf.astype(jnp.bfloat16), fresh(1), NN)
        out_ref[i, :PER_SEQ, :] = own_head(o).astype(jnp.bfloat16)


def decode_partials(lens, me, queries, cache, fresh):
    per_step = 16
    return pl.pallas_call(
        functools.partial(decode_kernel, per_step=per_step),
        grid_spec=pltpu.PrefetchScalarGridSpec(
            num_scalar_prefetch=2,
            grid=(SEQS // per_step,),
            in_specs=[
                pl.BlockSpec((STEPS, per_step, HEADS, HEAD_DIM), lambda i, *_: (0, i, 0, 0)),
                pl.BlockSpec((2, per_step, SLOTS, KV_HEADS * HEAD_DIM), lambda i, *_: (0, i, 0, 0)),
                pl.BlockSpec((STEPS, 2, 16, KV_HEADS * HEAD_DIM), lambda i, lens, me: (0, 0, me[0] // 16, 0)),
            ],
            out_specs=pl.BlockSpec((per_step, PACKED, HEAD_DIM), lambda i, *_: (i, 0, 0)),
        ),
        out_shape=jax.ShapeDtypeStruct((SEQS, PACKED, HEAD_DIM), jnp.bfloat16),
        compiler_params=pltpu.CompilerParams(vmem_limit_bytes=62 * 1024 * 1024),
        cost_estimate=pl.CostEstimate(flops=70_000_000, bytes_accessed=5_500_000, transcendentals=262144),
        name="decode_partials",
    )(lens, me, queries, cache, fresh)


def join_kernel(in_ref, out_ref, coef):
    peaks, totals = [], []
    for i in range(SEQS):
        st = in_ref[i, PER_SEQ:, :].astype(jnp.float32)
        peaks.append(st[0:1] + st[1:2])
        totals.append(st[2:3] + st[3:4])
    top = functools.reduce(jnp.maximum, peaks)
    scales = [jnp.exp2(m - top) for m in peaks]
    total = functools.reduce(jnp.add, [a * b for a, b in zip(scales, totals)])
    coef[...] = jnp.zeros_like(coef)
    for i in range(SEQS):
        coef[i : i + 1, :] = scales[i] / total
    columns = jnp.transpose(coef[...])
    acc = jnp.zeros((PER_SEQ, HEAD_DIM), jnp.float32)
    for i in range(SEQS):
        acc = acc + in_ref[i, :PER_SEQ, :].astype(jnp.float32) * columns[:PER_SEQ, i : i + 1]
    acc = acc.astype(jnp.bfloat16)
    for i in range(SEQS):
        out_ref[i] = acc


def join_shares(shares):
    return pl.pallas_call(
        join_kernel,
        out_shape=jax.ShapeDtypeStruct((SEQS, PER_SEQ, HEAD_DIM), jnp.bfloat16),
        in_specs=[pl.BlockSpec(memory_space=pltpu.VMEM)],
        out_specs=pl.BlockSpec(memory_space=pltpu.VMEM),
        scratch_shapes=[pltpu.VMEM((HEAD_DIM, HEAD_DIM), jnp.float32)],
        cost_estimate=pl.CostEstimate(flops=1_000_000, bytes_accessed=1_200_000, transcendentals=4096),
        name="join_shares",
    )(shares)


def block_kernel(doc_ref, kv_ref, out_ref):
    lane = lax.rem(lax.broadcasted_iota(jnp.int32, (16, KV_HEADS * HEAD_DIM), 1), HEAD_DIM)
    row = jnp.zeros((16, KV_HEADS * HEAD_DIM), jnp.float32)
    for d in range(1, 4):
        below = jnp.sum((doc_ref[...] < d).astype(jnp.float32), axis=1, keepdims=True)
        row = jnp.where(lane == d - 1, below, row)
    out_ref[0, 0 : 2 * ROWS, :] = kv_ref[...]
    out_ref[0, 2 * ROWS :, :] = row.astype(jnp.bfloat16)


def make_block(doc, key_values):
    vmem = pl.BlockSpec(memory_space=pltpu.VMEM)
    return pl.pallas_call(
        block_kernel,
        out_shape=jax.ShapeDtypeStruct((1, BLOCK, KV_HEADS * HEAD_DIM), jnp.bfloat16),
        in_specs=[vmem, vmem],
        out_specs=vmem,
        cost_estimate=pl.CostEstimate(flops=1000, bytes_accessed=400_000, transcendentals=0),
        name="make_block",
    )(doc, key_values)


def block_valid(y, xh, z, kind):
    across = (xh == 1) | (y >= 2)
    if kind == "own":
        return [y >= 0]
    if kind == "row":
        return [y >= 1]
    if kind == "far_row":
        return [y >= 1] * 4
    if kind == "back":
        return [y >= 2]
    if kind == "across":
        return [across]
    bit = 1 << (kind.bit_length() - 1)
    return [((z & bit) != 0) | (y >= 2), across]


COUNT = {"own": 1, "row": 1, "far_row": 4, "back": 1, "across": 1, 1: 2, 2: 2, 3: 2}


def prefill_kernel(me_ref, q_ref, own_info_ref, *refs, sources, first, last):
    blocks, rest = refs[: len(sources)], refs[len(sources) :]
    state_in = None
    if not first:
        state_in, rest = rest[0], rest[1:]
    out_ref, rest = rest[0], rest[1:]
    if last:
        state, rest = rest[0], rest[1:]
    else:
        state = out_ref.at[0]
    keys_ref, values_ref, queries_ref = rest
    step = pl.program_id(0)
    y, xh, z = me_ref[0] // 8, lax.rem(me_ref[0] // 4, 2), lax.rem(me_ref[0], 4)
    places = [(r, b) for r, source in enumerate(sources) for b in range(COUNT[source])]
    n = len(places)

    @pl.when(step == 0)
    def _():
        row = lax.broadcasted_iota(jnp.int32, (ROWS, HEAD_DIM), 0)
        lane = lax.broadcasted_iota(jnp.int32, (ROWS, HEAD_DIM), 1)

        def documents(info):
            t = info.astype(jnp.float32)[0:1, :].astype(jnp.int32)
            return sum((row >= t[:, d : d + 1]).astype(jnp.int32) for d in range(3))

        valid = []
        for source in sources:
            valid += block_valid(y, xh, z, source)
        for at, (r, b) in enumerate(places):
            doc = jnp.where(valid[at], documents(blocks[r][b, 2 * ROWS :, :]), HIDDEN_KEY)
            keys_ref[at * ROWS : (at + 1) * ROWS, HEAD_DIM:] = (lane == doc).astype(jnp.bfloat16)
        other = (lane <= HIDDEN_KEY) & (lane != documents(own_info_ref[0]))
        other = jnp.where(other, HIDDEN, 0.0).astype(jnp.bfloat16)
        for j in range(FUSED):
            queries_ref[j * ROWS : (j + 1) * ROWS, HEAD_DIM:] = other

    for at, (r, b) in enumerate(places):
        on = slice(at * ROWS, (at + 1) * ROWS)
        keys_ref[on, :HEAD_DIM] = blocks[r][b, 0:ROWS, :]
        values_ref[on, :] = blocks[r][b, ROWS : 2 * ROWS, :]
    for j in range(FUSED):
        queries_ref[j * ROWS : (j + 1) * ROWS, :HEAD_DIM] = q_ref[:, j * HEAD_DIM : (j + 1) * HEAD_DIM]

    def scores(lo, hi):
        return dot(keys_ref[lo * ROWS : hi * ROWS, :], queries_ref[...], NT)

    def own_scores():
        key = lax.broadcasted_iota(jnp.int32, (ROWS, LANES), 0)
        query = lax.rem(lax.broadcasted_iota(jnp.int32, (1, LANES), 1), ROWS)
        return jnp.where(key <= query, scores(0, 1), HIDDEN)

    def weighted(lo, hi, p):
        return dot(values_ref[lo * ROWS : hi * ROWS, :], p.astype(jnp.bfloat16), TN)

    def put(peak, total, summed):
        state[0:HEAD_DIM, :] = summed
        state[HEAD_DIM : HEAD_DIM + 8, :] = jnp.broadcast_to(peak, (8, LANES))
        state[HEAD_DIM + 8 :, :] = jnp.broadcast_to(total, (8, LANES))

    if first:
        s = own_scores()
        peak = jnp.max(s, axis=0, keepdims=True)
        p = jnp.exp2((s - peak) * TO_LOG2)
        total, summed = jnp.sum(p, axis=0, keepdims=True), weighted(0, 1, p)
    else:
        peak = state_in[0, HEAD_DIM : HEAD_DIM + 1, :]
        total = state_in[0, HEAD_DIM + 8 : HEAD_DIM + 9, :]
        summed = state_in[0, 0:HEAD_DIM, :]
    lo = 1 if first else 0
    p = jnp.exp2(scores(lo, n) * TO_LOG2 - peak * TO_LOG2)
    total = total + jnp.sum(p, axis=0, keepdims=True)
    put(peak, total, summed + weighted(lo, n, p))

    @pl.when(jnp.logical_not(jnp.max(total) < TOO_LARGE))
    def _():
        s = scores(0, n)
        if first:
            s = jnp.concatenate([own_scores(), s[ROWS:]], axis=0)
        peak = jnp.max(s, axis=0, keepdims=True)
        if not first:
            old = state_in[0, HEAD_DIM : HEAD_DIM + 1, :]
            peak = jnp.maximum(old, peak)
        p = jnp.exp2((s - peak) * TO_LOG2)
        total, summed = jnp.sum(p, axis=0, keepdims=True), weighted(0, n, p)
        if not first:
            factor = jnp.exp2((old - peak) * TO_LOG2)
            total = total + state_in[0, HEAD_DIM + 8 : HEAD_DIM + 9, :] * factor
            summed = summed + state_in[0, 0:HEAD_DIM, :] * factor
        put(peak, total, summed)

    if last:
        out = state[0:HEAD_DIM, :] / state[HEAD_DIM + 8 : HEAD_DIM + 9, :]
        out = jnp.transpose(out).astype(jnp.bfloat16)
        for j in range(FUSED):
            out_ref[:, j * HEAD_DIM : (j + 1) * HEAD_DIM] = out[j * ROWS : (j + 1) * ROWS]


def prefill_part(me, queries, own, blocks, sources, state, last, name):
    first = state is None
    n = sum(COUNT[source] for source in sources)
    steps = HEADS // FUSED
    per_kv = steps // KV_HEADS
    q_spec = pl.BlockSpec((ROWS, FUSED * HEAD_DIM), lambda i, *_: (0, i))
    state_spec = pl.BlockSpec((1, STATE, LANES), lambda i, *_: (i, 0, 0))
    in_specs = [q_spec, pl.BlockSpec((1, 16, HEAD_DIM), lambda i, *_: (0, 2 * ROWS // 16, 0))]
    in_specs += [
        pl.BlockSpec((COUNT[source], BLOCK, HEAD_DIM), lambda i, *_: (0, 0, i // per_kv)) for source in sources
    ]
    operands = [me, queries, own, *blocks]
    scratch = []
    if not first:
        in_specs.append(state_spec)
        operands.append(state)
    if last:
        out_shape = jax.ShapeDtypeStruct((ROWS, HEADS * HEAD_DIM), jnp.bfloat16)
        out_spec = q_spec
        scratch.append(pltpu.VMEM((STATE, LANES), jnp.float32))
    else:
        out_shape = jax.ShapeDtypeStruct((steps, STATE, LANES), jnp.float32)
        out_spec = state_spec
    scratch += [
        pltpu.VMEM((n * ROWS, 2 * HEAD_DIM), jnp.bfloat16),
        pltpu.VMEM((n * ROWS, HEAD_DIM), jnp.bfloat16),
        pltpu.VMEM((LANES, 2 * HEAD_DIM), jnp.bfloat16),
    ]
    return pl.pallas_call(
        functools.partial(prefill_kernel, sources=sources, first=first, last=last),
        grid_spec=pltpu.PrefetchScalarGridSpec(
            num_scalar_prefetch=1,
            grid=(steps,),
            in_specs=in_specs,
            out_specs=out_spec,
            scratch_shapes=scratch,
        ),
        out_shape=out_shape,
        compiler_params=pltpu.CompilerParams(vmem_limit_bytes=62 * 1024 * 1024),
        cost_estimate=pl.CostEstimate(
            flops=4 * n * ROWS * ROWS * HEADS * HEAD_DIM, bytes_accessed=4_000_000, transcendentals=0
        ),
        name=name,
    )(*operands)


SIDE = (2, 1, 3)


def local(prefill_queries, prefill_key_values, fill_doc, decode_queries, step_key_values, stored_key_values, cached_len):
    y, xh, z = [lax.axis_index(axis).astype(jnp.int32) for axis in CTX]
    me = (y * 2 + xh) * 4 + z

    own = make_block(fill_doc[None], prefill_key_values.reshape(2 * ROWS, KV_HEADS * HEAD_DIM))
    back1 = lax.ppermute(own, "y", [(i, i + 1) for i in range(3)])
    back2 = lax.ppermute(own, "y", [(i, i + 2) for i in range(2)])
    queries = decode_queries.reshape(STEPS, SEQS, HEADS, HEAD_DIM)
    shares = decode_partials(cached_len, me[None], queries, stored_key_values, step_key_values)

    back1, back2, shares = lax.optimization_barrier((back1, back2, shares))
    row = [back1] + [lax.ppermute(back1, "z", [(i, i ^ k) for i in range(4)]) for k in SIDE]
    across = lax.ppermute(jnp.where(xh == 0, own, back2), "xh", [(0, 1), (1, 0)])
    far_row = lax.ppermute(jnp.concatenate(row, axis=0), "xh", [(0, 1), (1, 0)])
    packs = {bit: jnp.concatenate([jnp.where((z & bit) == 0, own, back2), across], axis=0) for bit in (1, 2)}
    packs, shares = lax.optimization_barrier((packs, shares))
    side = {k: lax.ppermute(packs[min(k, 2)], "z", [(i, i ^ k) for i in range(4)]) for k in SIDE}

    shares = lax.all_to_all(shares, CTX, 0, 0)
    sources = ("own",) + ("row",) * 4 + ("back", "across")
    blocks = [own, *row, back2, across]
    state = prefill_part(me[None], prefill_queries, own, blocks, sources, None, False, "prefill_first")
    shares, state = lax.optimization_barrier((shares, state))
    spread = lax.all_to_all(join_shares(shares), CTX, 0, 0)
    sources = ("far_row",) + SIDE
    blocks = [far_row] + [side[k] for k in SIDE]
    fill_out = prefill_part(me[None], prefill_queries, own, blocks, sources, state, True, "prefill_last")
    spread, fill_out = lax.optimization_barrier((spread, fill_out))
    step_out = spread.reshape(SEQS, STEPS, HEADS, HEAD_DIM).transpose(1, 0, 2, 3)
    return fill_out, step_out.reshape(STEPS, SEQS, HEADS * HEAD_DIM)


def solution(mesh):
    fine = Mesh(mesh.devices.reshape(4, 2, 4, 2, 2), ("y", "xh", "z", "xl", "c"))
    tp = ("xl", "c")
    placed = (
        P(CTX, tp),
        P(None, CTX, tp),
        P(CTX),
        P(None, None, tp),
        P(None, None, None, tp),
        P(None, None, CTX, tp),
        P(),
    )
    return jax.shard_map(
        local,
        mesh=fine,
        in_specs=placed,
        out_specs=(P(CTX, tp), P(None, None, tp)),
        check_vma=False,
    )
```

```python
import functools

import jax
import jax.numpy as jnp
from jax import lax
from jax.experimental import pallas as pl
from jax.experimental.pallas import tpu as pltpu
from jax.sharding import Mesh
from jax.sharding import PartitionSpec as P

HEAD_DIM = 128
GROUP = 8
STEPS = 4
SEQS = 32
SLOTS = 128
ROWS = 192
KV_HEADS = 2
HEADS = KV_HEADS * GROUP
PER_KV = STEPS * GROUP
PER_SEQ = STEPS * HEADS
PACKED = PER_SEQ + 16
FUSED = 8
LANES = FUSED * ROWS
BLOCK = 2 * ROWS + 16
STATE = HEAD_DIM + 16
HIDDEN = -1e30
FLOOR = -1e20
NOWHERE = -1000000
TOO_LARGE = 2.0**100
HIDDEN_KEY = 4
TO_LOG2 = HEAD_DIM**-0.5 * 1.4426950408889634
CTX = ("y", "xh", "z")
PLANE = ("xh", "z")

NT = (((1,), (1,)), ((), ()))
TN = (((0,), (0,)), ((), ()))
NN = (((1,), (0,)), ((), ()))


def dot(a, b, dims):
    return lax.dot_general(a, b, dims, preferred_element_type=jnp.float32)


def halves(value):
    high = value.astype(jnp.bfloat16).astype(jnp.float32)
    return high, (value - high).astype(jnp.bfloat16).astype(jnp.float32)


def decode_kernel(len_ref, me_ref, q_ref, kv_ref, step_ref, out_ref, rows_ref, *, per_step):
    base = pl.program_id(0) * per_step
    me = me_ref[0]
    lane = lax.broadcasted_iota(jnp.int32, (PER_SEQ, SLOTS), 1)
    tile_row = lax.broadcasted_iota(jnp.int32, (16, HEAD_DIM), 0)
    tile_lane = lax.broadcasted_iota(jnp.int32, (16, HEAD_DIM), 1)
    pick = ((tile_row == tile_lane) & (tile_row < 4)).astype(jnp.bfloat16)
    row = lax.broadcasted_iota(jnp.int32, (PER_SEQ, HEAD_DIM), 0)
    second = lax.rem(row, HEADS) >= GROUP

    for t in range(STEPS):
        for h in range(HEADS):
            at = (t * HEADS + h) * per_step
            rows_ref[at : at + per_step, :] = q_ref[t, :, h * HEAD_DIM : (h + 1) * HEAD_DIM].astype(jnp.float32)

    def queries_of(i):
        q = rows_ref[pl.ds(i, PER_SEQ, stride=per_step), :].astype(jnp.bfloat16)
        none = jnp.zeros_like(q)
        return jnp.concatenate([jnp.where(second, none, q), jnp.where(second, q, none)], axis=1)

    def scores(i):
        return jnp.where(
            lane < len_ref[base + i] - me * SLOTS, dot(queries_of(i), kv_ref[0, i], NT) * TO_LOG2, HIDDEN
        )

    def own_head(o):
        return jnp.where(second, o[:, HEAD_DIM:], o[:, :HEAD_DIM])

    def pack_stats(m_hi, m_lo, total):
        l_hi, l_lo = halves(total)
        at = lax.broadcasted_iota(jnp.int32, (total.shape[0], HEAD_DIM), 1)
        st = jnp.where(at == 0, m_hi, jnp.where(at == 1, m_lo, jnp.where(at == 2, l_hi, l_lo)))
        return dot(pick, st.astype(jnp.bfloat16), NT)

    s = jnp.concatenate([scores(i) for i in range(per_step)], axis=0)
    m_hi, m_lo = halves(jnp.maximum(jnp.max(s, axis=1, keepdims=True), FLOOR))
    p = jnp.exp2(s - (m_hi + m_lo))
    tile = pack_stats(m_hi, m_lo, jnp.sum(p, axis=1, keepdims=True))
    p = p.astype(jnp.bfloat16)
    for i in range(per_step):
        o = dot(p[i * PER_SEQ : (i + 1) * PER_SEQ], kv_ref[1, i], NN)
        out_ref[i, :PER_SEQ, :] = own_head(o).astype(jnp.bfloat16)
    for i in range(0, per_step, 2):
        pair = tile[:, i * PER_SEQ : (i + 2) * PER_SEQ]
        out_ref[i, PER_SEQ:, :] = pair.astype(jnp.bfloat16)
        swapped = jnp.concatenate([pair[:, PER_SEQ:], pair[:, :PER_SEQ]], axis=1)
        out_ref[i + 1, PER_SEQ:, :] = swapped.astype(jnp.bfloat16)

    @pl.when((me >= base) & (me < base + per_step))
    def _():
        i = me - base
        chosen = lax.broadcasted_iota(jnp.int32, (16, KV_HEADS * HEAD_DIM), 0) == lax.rem(me, 16)

        def fresh(kind):
            rows = [
                jnp.sum(jnp.where(chosen, step_ref[t, kind].astype(jnp.float32), 0.0), axis=0, keepdims=True)
                for t in range(STEPS)
            ]
            rows.append(jnp.zeros((HEAD_DIM - STEPS, KV_HEADS * HEAD_DIM), jnp.float32))
            return jnp.concatenate(rows, axis=0).astype(jnp.bfloat16)

        s = scores(i)
        f = jnp.where(lane <= row // HEADS, dot(queries_of(i), fresh(0), NT) * TO_LOG2, HIDDEN)
        m_hi, m_lo = halves(jnp.maximum(jnp.max(s, axis=1, keepdims=True), jnp.max(f, axis=1, keepdims=True)))
        p = jnp.exp2(s - (m_hi + m_lo))
        pf = jnp.exp2(f - (m_hi + m_lo))
        total = jnp.sum(p, axis=1, keepdims=True) + jnp.sum(pf, axis=1, keepdims=True)
        stats = [jnp.concatenate([x, jnp.zeros_like(x)], axis=0) for x in (m_hi, m_lo, total)]
        out_ref[i, PER_SEQ:, :] = pack_stats(*stats).astype(jnp.bfloat16)
        o = dot(p.astype(jnp.bfloat16), kv_ref[1, i], NN) + dot(pf.astype(jnp.bfloat16), fresh(1), NN)
        out_ref[i, :PER_SEQ, :] = own_head(o).astype(jnp.bfloat16)


def decode_partials(lens, me, queries, cache, fresh):
    per_step = 16
    return pl.pallas_call(
        functools.partial(decode_kernel, per_step=per_step),
        grid_spec=pltpu.PrefetchScalarGridSpec(
            num_scalar_prefetch=2,
            grid=(SEQS // per_step,),
            in_specs=[
                pl.BlockSpec((STEPS, per_step, HEADS * HEAD_DIM), lambda i, *_: (0, i, 0)),
                pl.BlockSpec((2, per_step, SLOTS, KV_HEADS * HEAD_DIM), lambda i, *_: (0, i, 0, 0)),
                pl.BlockSpec((STEPS, 2, 16, KV_HEADS * HEAD_DIM), lambda i, lens, me: (0, 0, me[0] // 16, 0)),
            ],
            out_specs=pl.BlockSpec((per_step, PACKED, HEAD_DIM), lambda i, *_: (i, 0, 0)),
            scratch_shapes=[pltpu.VMEM((PER_SEQ * per_step, HEAD_DIM), jnp.float32)],
        ),
        out_shape=jax.ShapeDtypeStruct((SEQS, PACKED, HEAD_DIM), jnp.bfloat16),
        compiler_params=pltpu.CompilerParams(vmem_limit_bytes=62 * 1024 * 1024),
        cost_estimate=pl.CostEstimate(flops=70_000_000, bytes_accessed=5_500_000, transcendentals=262144),
        name="decode_partials",
    )(lens, me, queries, cache, fresh)


def join_kernel(in_ref, out_ref, coef, joined):
    peaks, totals = [], []
    for i in range(SEQS):
        st = in_ref[i, PER_SEQ:, :].astype(jnp.float32)
        peaks.append(st[0:1] + st[1:2])
        totals.append(st[2:3] + st[3:4])
    top = functools.reduce(jnp.maximum, peaks)
    scales = [jnp.exp2(m - top) for m in peaks]
    total = functools.reduce(jnp.add, [a * b for a, b in zip(scales, totals)])
    coef[...] = jnp.zeros_like(coef)
    for i in range(SEQS):
        coef[i : i + 1, :] = scales[i] / total
    columns = jnp.transpose(coef[...])
    acc = jnp.zeros((PER_SEQ, HEAD_DIM), jnp.float32)
    for i in range(SEQS):
        acc = acc + in_ref[i, :PER_SEQ, :].astype(jnp.float32) * columns[:PER_SEQ, i : i + 1]
    joined[...] = acc
    heads = [joined[pl.ds(h, STEPS, stride=HEADS), :] for h in range(HEADS)]
    out = jnp.concatenate(heads, axis=1).astype(jnp.bfloat16)
    for i in range(SEQS):
        out_ref[i] = out


def join_shares(shares):
    return pl.pallas_call(
        join_kernel,
        out_shape=jax.ShapeDtypeStruct((SEQS, STEPS, HEADS * HEAD_DIM), jnp.bfloat16),
        in_specs=[pl.BlockSpec(memory_space=pltpu.VMEM)],
        out_specs=pl.BlockSpec(memory_space=pltpu.VMEM),
        scratch_shapes=[pltpu.VMEM((HEAD_DIM, HEAD_DIM), jnp.float32), pltpu.VMEM((PER_SEQ, HEAD_DIM), jnp.float32)],
        compiler_params=pltpu.CompilerParams(vmem_limit_bytes=8 * 1024 * 1024),
        cost_estimate=pl.CostEstimate(flops=1_000_000, bytes_accessed=1_200_000, transcendentals=4096),
        name="join_shares",
    )(shares)


def block_kernel(doc_ref, kv_ref, out_ref):
    lane = lax.rem(lax.broadcasted_iota(jnp.int32, (16, KV_HEADS * HEAD_DIM), 1), HEAD_DIM)
    row = jnp.zeros((16, KV_HEADS * HEAD_DIM), jnp.float32)
    for d in range(1, 4):
        below = jnp.sum((doc_ref[...] < d).astype(jnp.float32), axis=1, keepdims=True)
        row = jnp.where(lane == d - 1, below, row)
    out_ref[0, 0 : 2 * ROWS, :] = kv_ref[...]
    out_ref[0, 2 * ROWS :, :] = row.astype(jnp.bfloat16)


def make_block(doc, key_values):
    vmem = pl.BlockSpec(memory_space=pltpu.VMEM)
    return pl.pallas_call(
        block_kernel,
        out_shape=jax.ShapeDtypeStruct((1, BLOCK, KV_HEADS * HEAD_DIM), jnp.bfloat16),
        in_specs=[vmem, vmem],
        out_specs=vmem,
        cost_estimate=pl.CostEstimate(flops=1000, bytes_accessed=400_000, transcendentals=0),
        name="make_block",
    )(doc, key_values)


def block_valid(y, xh, z, kind):
    across = (xh == 1) | (y >= 2)
    if kind == "own":
        return [y >= 0]
    if kind == "row":
        return [y >= 1]
    if kind == "far_row":
        return [y >= 1] * 4
    if kind == "back":
        return [y >= 2]
    if kind == "across":
        return [across]
    bit = 1 << (kind.bit_length() - 1)
    return [((z & bit) != 0) | (y >= 2), across]


COUNT = {"own": 1, "row": 1, "far_row": 4, "back": 1, "across": 1, 1: 2, 2: 2, 3: 2}


def prefill_kernel(me_ref, q_ref, own_info_ref, *refs, sources, first, last):
    blocks, rest = refs[: len(sources)], refs[len(sources) :]
    state_in = None
    if not first:
        state_in, rest = rest[0], rest[1:]
    out_ref, rest = rest[0], rest[1:]
    if last:
        state, rest = rest[0], rest[1:]
    else:
        state = out_ref.at[0]
    keys_ref, values_ref, queries_ref = rest
    step = pl.program_id(0)
    y, xh, z = me_ref[0] // 8, lax.rem(me_ref[0] // 4, 2), lax.rem(me_ref[0], 4)
    places = [(r, b) for r, source in enumerate(sources) for b in range(COUNT[source])]
    n = len(places)

    @pl.when(step == 0)
    def _():
        row = lax.broadcasted_iota(jnp.int32, (ROWS, HEAD_DIM), 0)
        lane = lax.broadcasted_iota(jnp.int32, (ROWS, HEAD_DIM), 1)

        def documents(info):
            t = info.astype(jnp.float32)[0:1, :].astype(jnp.int32)
            return sum((row >= t[:, d : d + 1]).astype(jnp.int32) for d in range(3))

        valid = []
        for source in sources:
            valid += block_valid(y, xh, z, source)
        for at, (r, b) in enumerate(places):
            doc = jnp.where(valid[at], documents(blocks[r][b, 2 * ROWS :, :]), HIDDEN_KEY)
            keys_ref[at * ROWS : (at + 1) * ROWS, HEAD_DIM:] = (lane == doc).astype(jnp.bfloat16)
        other = (lane <= HIDDEN_KEY) & (lane != documents(own_info_ref[0]))
        other = jnp.where(other, HIDDEN, 0.0).astype(jnp.bfloat16)
        for j in range(FUSED):
            queries_ref[j * ROWS : (j + 1) * ROWS, HEAD_DIM:] = other

    for at, (r, b) in enumerate(places):
        on = slice(at * ROWS, (at + 1) * ROWS)
        keys_ref[on, :HEAD_DIM] = blocks[r][b, 0:ROWS, :]
        values_ref[on, :] = blocks[r][b, ROWS : 2 * ROWS, :]
    for j in range(FUSED):
        queries_ref[j * ROWS : (j + 1) * ROWS, :HEAD_DIM] = q_ref[:, j * HEAD_DIM : (j + 1) * HEAD_DIM]

    def scores(lo, hi):
        return dot(keys_ref[lo * ROWS : hi * ROWS, :], queries_ref[...], NT)

    def own_scores():
        key = lax.broadcasted_iota(jnp.int32, (ROWS, LANES), 0)
        query = lax.rem(lax.broadcasted_iota(jnp.int32, (1, LANES), 1), ROWS)
        return jnp.where(key <= query, scores(0, 1), HIDDEN)

    def weighted(lo, hi, p):
        return dot(values_ref[lo * ROWS : hi * ROWS, :], p.astype(jnp.bfloat16), TN)

    def put(peak, total, summed):
        state[0:HEAD_DIM, :] = summed
        state[HEAD_DIM : HEAD_DIM + 8, :] = jnp.broadcast_to(peak, (8, LANES))
        state[HEAD_DIM + 8 :, :] = jnp.broadcast_to(total, (8, LANES))

    if first:
        s = own_scores()
        peak = jnp.max(s, axis=0, keepdims=True)
        p = jnp.exp2((s - peak) * TO_LOG2)
        total, summed = jnp.sum(p, axis=0, keepdims=True), weighted(0, 1, p)
    else:
        peak = state_in[0, HEAD_DIM : HEAD_DIM + 1, :]
        total = state_in[0, HEAD_DIM + 8 : HEAD_DIM + 9, :]
        summed = state_in[0, 0:HEAD_DIM, :]
    lo = 1 if first else 0
    p = jnp.exp2(scores(lo, n) * TO_LOG2 - peak * TO_LOG2)
    total = total + jnp.sum(p, axis=0, keepdims=True)
    put(peak, total, summed + weighted(lo, n, p))

    @pl.when(jnp.logical_not(jnp.max(total) < TOO_LARGE))
    def _():
        s = scores(0, n)
        if first:
            s = jnp.concatenate([own_scores(), s[ROWS:]], axis=0)
        peak = jnp.max(s, axis=0, keepdims=True)
        if not first:
            old = state_in[0, HEAD_DIM : HEAD_DIM + 1, :]
            peak = jnp.maximum(old, peak)
        p = jnp.exp2((s - peak) * TO_LOG2)
        total, summed = jnp.sum(p, axis=0, keepdims=True), weighted(0, n, p)
        if not first:
            factor = jnp.exp2((old - peak) * TO_LOG2)
            total = total + state_in[0, HEAD_DIM + 8 : HEAD_DIM + 9, :] * factor
            summed = summed + state_in[0, 0:HEAD_DIM, :] * factor
        put(peak, total, summed)

    if last:
        out = state[0:HEAD_DIM, :] / state[HEAD_DIM + 8 : HEAD_DIM + 9, :]
        out = jnp.transpose(out).astype(jnp.bfloat16)
        for j in range(FUSED):
            out_ref[:, j * HEAD_DIM : (j + 1) * HEAD_DIM] = out[j * ROWS : (j + 1) * ROWS]


def prefill_part(me, queries, own, blocks, sources, state, last, name):
    first = state is None
    n = sum(COUNT[source] for source in sources)
    steps = HEADS // FUSED
    per_kv = steps // KV_HEADS
    q_spec = pl.BlockSpec((ROWS, FUSED * HEAD_DIM), lambda i, *_: (0, i))
    state_spec = pl.BlockSpec((1, STATE, LANES), lambda i, *_: (i, 0, 0))
    in_specs = [q_spec, pl.BlockSpec((1, 16, HEAD_DIM), lambda i, *_: (0, 2 * ROWS // 16, 0))]
    in_specs += [
        pl.BlockSpec((COUNT[source], BLOCK, HEAD_DIM), lambda i, *_: (0, 0, i // per_kv)) for source in sources
    ]
    operands = [me, queries, own, *blocks]
    scratch = []
    if not first:
        in_specs.append(state_spec)
        operands.append(state)
    if last:
        out_shape = jax.ShapeDtypeStruct((ROWS, HEADS * HEAD_DIM), jnp.bfloat16)
        out_spec = q_spec
        scratch.append(pltpu.VMEM((STATE, LANES), jnp.float32))
    else:
        out_shape = jax.ShapeDtypeStruct((steps, STATE, LANES), jnp.float32)
        out_spec = state_spec
    scratch += [
        pltpu.VMEM((n * ROWS, 2 * HEAD_DIM), jnp.bfloat16),
        pltpu.VMEM((n * ROWS, HEAD_DIM), jnp.bfloat16),
        pltpu.VMEM((LANES, 2 * HEAD_DIM), jnp.bfloat16),
    ]
    return pl.pallas_call(
        functools.partial(prefill_kernel, sources=sources, first=first, last=last),
        grid_spec=pltpu.PrefetchScalarGridSpec(
            num_scalar_prefetch=1,
            grid=(steps,),
            in_specs=in_specs,
            out_specs=out_spec,
            scratch_shapes=scratch,
        ),
        out_shape=out_shape,
        compiler_params=pltpu.CompilerParams(vmem_limit_bytes=62 * 1024 * 1024),
        cost_estimate=pl.CostEstimate(
            flops=4 * n * ROWS * ROWS * HEADS * HEAD_DIM, bytes_accessed=4_000_000, transcendentals=0
        ),
        name=name,
    )(*operands)


SIDE = (2, 1, 3)


def local(prefill_queries, prefill_key_values, fill_doc, decode_queries, step_key_values, stored_key_values, cached_len):
    y, xh, z = [lax.axis_index(axis).astype(jnp.int32) for axis in CTX]
    me = (y * 2 + xh) * 4 + z

    own = make_block(fill_doc[None], prefill_key_values.reshape(2 * ROWS, KV_HEADS * HEAD_DIM))
    back1 = lax.ppermute(own, "y", [(i, i + 1) for i in range(3)])
    back2 = lax.ppermute(own, "y", [(i, i + 2) for i in range(2)])
    shares = decode_partials(cached_len, me[None], decode_queries, stored_key_values, step_key_values)

    back1, back2, shares = lax.optimization_barrier((back1, back2, shares))
    row = [back1] + [lax.ppermute(back1, "z", [(i, i ^ k) for i in range(4)]) for k in SIDE]
    across = lax.ppermute(jnp.where(xh == 0, own, back2), "xh", [(0, 1), (1, 0)])
    far_row = lax.ppermute(jnp.concatenate(row, axis=0), "xh", [(0, 1), (1, 0)])
    packs = {bit: jnp.concatenate([jnp.where((z & bit) == 0, own, back2), across], axis=0) for bit in (1, 2)}
    packs, shares = lax.optimization_barrier((packs, shares))
    side = {k: lax.ppermute(packs[min(k, 2)], "z", [(i, i ^ k) for i in range(4)]) for k in SIDE}

    shares = lax.all_to_all(shares, CTX, 0, 0)
    sources = ("own",) + ("row",) * 4 + ("back", "across")
    blocks = [own, *row, back2, across]
    state = prefill_part(me[None], prefill_queries, own, blocks, sources, None, False, "prefill_first")
    shares, state = lax.optimization_barrier((shares, state))
    spread = lax.all_to_all(join_shares(shares), CTX, 0, 0)
    sources = ("far_row",) + SIDE
    blocks = [far_row] + [side[k] for k in SIDE]
    fill_out = prefill_part(me[None], prefill_queries, own, blocks, sources, state, True, "prefill_last")
    spread, fill_out = lax.optimization_barrier((spread, fill_out))
    return fill_out, spread.transpose(1, 0, 2)


def solution(mesh):
    fine = Mesh(mesh.devices.reshape(4, 2, 4, 2, 2), ("y", "xh", "z", "xl", "c"))
    tp = ("xl", "c")
    placed = (
        P(CTX, tp),
        P(None, CTX, tp),
        P(CTX),
        P(None, None, tp),
        P(None, None, None, tp),
        P(None, None, CTX, tp),
        P(),
    )
    return jax.shard_map(
        local,
        mesh=fine,
        in_specs=placed,
        out_specs=(P(CTX, tp), P(None, None, tp)),
        check_vma=False,
    )
```

```python
import functools

import jax
import jax.numpy as jnp
from jax import lax
from jax.experimental import pallas as pl
from jax.experimental.pallas import tpu as pltpu
from jax.sharding import Mesh
from jax.sharding import PartitionSpec as P

HEAD_DIM = 128
GROUP = 8
STEPS = 4
SEQS = 32
SLOTS = 128
ROWS = 192
KV_HEADS = 2
HEADS = KV_HEADS * GROUP
PER_KV = STEPS * GROUP
PER_SEQ = STEPS * HEADS
PACKED = PER_SEQ + 16
FUSED = 8
LANES = FUSED * ROWS
BLOCK = 2 * ROWS + 16
STATE = HEAD_DIM + 16
HIDDEN = -1e30
FLOOR = -1e20
NOWHERE = -1000000
TOO_LARGE = 2.0**100
HIDDEN_KEY = 4
TO_LOG2 = HEAD_DIM**-0.5 * 1.4426950408889634
CTX = ("y", "xh", "z")
PLANE = ("xh", "z")

NT = (((1,), (1,)), ((), ()))
TN = (((0,), (0,)), ((), ()))
NN = (((1,), (0,)), ((), ()))


def dot(a, b, dims):
    return lax.dot_general(a, b, dims, preferred_element_type=jnp.float32)


def halves(value):
    high = value.astype(jnp.bfloat16).astype(jnp.float32)
    return high, (value - high).astype(jnp.bfloat16).astype(jnp.float32)


def decode_kernel(len_ref, me_ref, q_ref, kv_ref, step_ref, out_ref, rows_ref, *, per_step):
    base = pl.program_id(0) * per_step
    me = me_ref[0]
    lane = lax.broadcasted_iota(jnp.int32, (PER_SEQ, SLOTS), 1)
    tile_row = lax.broadcasted_iota(jnp.int32, (16, HEAD_DIM), 0)
    tile_lane = lax.broadcasted_iota(jnp.int32, (16, HEAD_DIM), 1)
    pick = ((tile_row == tile_lane) & (tile_row < 4)).astype(jnp.bfloat16)
    row = lax.broadcasted_iota(jnp.int32, (PER_SEQ, HEAD_DIM), 0)
    second = lax.rem(row, HEADS) >= GROUP

    for t in range(STEPS):
        for h in range(HEADS):
            at = (t * HEADS + h) * per_step
            rows_ref[at : at + per_step, :] = q_ref[t, :, h * HEAD_DIM : (h + 1) * HEAD_DIM].astype(jnp.float32)

    def queries_of(i):
        q = rows_ref[pl.ds(i, PER_SEQ, stride=per_step), :].astype(jnp.bfloat16)
        none = jnp.zeros_like(q)
        return jnp.concatenate([jnp.where(second, none, q), jnp.where(second, q, none)], axis=1)

    def scores(i):
        return jnp.where(
            lane < len_ref[base + i] - me * SLOTS, dot(queries_of(i), kv_ref[0, i], NT) * TO_LOG2, HIDDEN
        )

    def own_head(o):
        return jnp.where(second, o[:, HEAD_DIM:], o[:, :HEAD_DIM])

    def pack_stats(m_hi, m_lo, total):
        l_hi, l_lo = halves(total)
        at = lax.broadcasted_iota(jnp.int32, (total.shape[0], HEAD_DIM), 1)
        st = jnp.where(at == 0, m_hi, jnp.where(at == 1, m_lo, jnp.where(at == 2, l_hi, l_lo)))
        return dot(pick, st.astype(jnp.bfloat16), NT)

    s = jnp.concatenate([scores(i) for i in range(per_step)], axis=0)
    m_hi, m_lo = halves(jnp.maximum(jnp.max(s, axis=1, keepdims=True), FLOOR))
    p = jnp.exp2(s - (m_hi + m_lo))
    tile = pack_stats(m_hi, m_lo, jnp.sum(p, axis=1, keepdims=True))
    p = p.astype(jnp.bfloat16)
    for i in range(per_step):
        o = dot(p[i * PER_SEQ : (i + 1) * PER_SEQ], kv_ref[1, i], NN)
        out_ref[i, :PER_SEQ, :] = own_head(o).astype(jnp.bfloat16)
    for i in range(0, per_step, 2):
        pair = tile[:, i * PER_SEQ : (i + 2) * PER_SEQ]
        out_ref[i, PER_SEQ:, :] = pair.astype(jnp.bfloat16)
        swapped = jnp.concatenate([pair[:, PER_SEQ:], pair[:, :PER_SEQ]], axis=1)
        out_ref[i + 1, PER_SEQ:, :] = swapped.astype(jnp.bfloat16)

    @pl.when((me >= base) & (me < base + per_step))
    def _():
        i = me - base
        chosen = lax.broadcasted_iota(jnp.int32, (16, KV_HEADS * HEAD_DIM), 0) == lax.rem(me, 16)

        def fresh(kind):
            rows = [
                jnp.sum(jnp.where(chosen, step_ref[t, kind].astype(jnp.float32), 0.0), axis=0, keepdims=True)
                for t in range(STEPS)
            ]
            rows.append(jnp.zeros((HEAD_DIM - STEPS, KV_HEADS * HEAD_DIM), jnp.float32))
            return jnp.concatenate(rows, axis=0).astype(jnp.bfloat16)

        s = scores(i)
        f = jnp.where(lane <= row // HEADS, dot(queries_of(i), fresh(0), NT) * TO_LOG2, HIDDEN)
        m_hi, m_lo = halves(jnp.maximum(jnp.max(s, axis=1, keepdims=True), jnp.max(f, axis=1, keepdims=True)))
        p = jnp.exp2(s - (m_hi + m_lo))
        pf = jnp.exp2(f - (m_hi + m_lo))
        total = jnp.sum(p, axis=1, keepdims=True) + jnp.sum(pf, axis=1, keepdims=True)
        stats = [jnp.concatenate([x, jnp.zeros_like(x)], axis=0) for x in (m_hi, m_lo, total)]
        out_ref[i, PER_SEQ:, :] = pack_stats(*stats).astype(jnp.bfloat16)
        o = dot(p.astype(jnp.bfloat16), kv_ref[1, i], NN) + dot(pf.astype(jnp.bfloat16), fresh(1), NN)
        out_ref[i, :PER_SEQ, :] = own_head(o).astype(jnp.bfloat16)


def decode_partials(lens, me, queries, cache, fresh):
    per_step = 16
    return pl.pallas_call(
        functools.partial(decode_kernel, per_step=per_step),
        grid_spec=pltpu.PrefetchScalarGridSpec(
            num_scalar_prefetch=2,
            grid=(SEQS // per_step,),
            in_specs=[
                pl.BlockSpec((STEPS, per_step, HEADS * HEAD_DIM), lambda i, *_: (0, i, 0)),
                pl.BlockSpec((2, per_step, SLOTS, KV_HEADS * HEAD_DIM), lambda i, *_: (0, i, 0, 0)),
                pl.BlockSpec((STEPS, 2, 16, KV_HEADS * HEAD_DIM), lambda i, lens, me: (0, 0, me[0] // 16, 0)),
            ],
            out_specs=pl.BlockSpec((per_step, PACKED, HEAD_DIM), lambda i, *_: (i, 0, 0)),
            scratch_shapes=[pltpu.VMEM((PER_SEQ * per_step, HEAD_DIM), jnp.float32)],
        ),
        out_shape=jax.ShapeDtypeStruct((SEQS, PACKED, HEAD_DIM), jnp.bfloat16),
        compiler_params=pltpu.CompilerParams(vmem_limit_bytes=62 * 1024 * 1024),
        cost_estimate=pl.CostEstimate(flops=70_000_000, bytes_accessed=5_500_000, transcendentals=262144),
        name="decode_partials",
    )(lens, me, queries, cache, fresh)


def join_kernel(in_ref, out_ref, coef, joined):
    peaks, totals = [], []
    for i in range(SEQS):
        st = in_ref[i, PER_SEQ:, :].astype(jnp.float32)
        peaks.append(st[0:1] + st[1:2])
        totals.append(st[2:3] + st[3:4])
    top = functools.reduce(jnp.maximum, peaks)
    scales = [jnp.exp2(m - top) for m in peaks]
    total = functools.reduce(jnp.add, [a * b for a, b in zip(scales, totals)])
    coef[...] = jnp.zeros_like(coef)
    for i in range(SEQS):
        coef[i : i + 1, :] = scales[i] / total
    columns = jnp.transpose(coef[...])
    acc = jnp.zeros((PER_SEQ, HEAD_DIM), jnp.float32)
    for i in range(SEQS):
        acc = acc + in_ref[i, :PER_SEQ, :].astype(jnp.float32) * columns[:PER_SEQ, i : i + 1]
    joined[...] = acc
    heads = [joined[pl.ds(h, STEPS, stride=HEADS), :] for h in range(HEADS)]
    out = jnp.concatenate(heads, axis=1).astype(jnp.bfloat16)
    for i in range(SEQS):
        out_ref[i] = out


def join_shares(shares):
    return pl.pallas_call(
        join_kernel,
        out_shape=jax.ShapeDtypeStruct((SEQS, STEPS, HEADS * HEAD_DIM), jnp.bfloat16),
        in_specs=[pl.BlockSpec(memory_space=pltpu.VMEM)],
        out_specs=pl.BlockSpec(memory_space=pltpu.VMEM),
        scratch_shapes=[pltpu.VMEM((HEAD_DIM, HEAD_DIM), jnp.float32), pltpu.VMEM((PER_SEQ, HEAD_DIM), jnp.float32)],
        compiler_params=pltpu.CompilerParams(vmem_limit_bytes=8 * 1024 * 1024),
        cost_estimate=pl.CostEstimate(flops=1_000_000, bytes_accessed=1_200_000, transcendentals=4096),
        name="join_shares",
    )(shares)


def block_kernel(doc_ref, kv_ref, out_ref):
    lane = lax.rem(lax.broadcasted_iota(jnp.int32, (16, KV_HEADS * HEAD_DIM), 1), HEAD_DIM)
    row = jnp.zeros((16, KV_HEADS * HEAD_DIM), jnp.float32)
    for d in range(1, 4):
        below = jnp.sum((doc_ref[...] < d).astype(jnp.float32), axis=1, keepdims=True)
        row = jnp.where(lane == d - 1, below, row)
    out_ref[0, 0 : 2 * ROWS, :] = kv_ref[...]
    out_ref[0, 2 * ROWS :, :] = row.astype(jnp.bfloat16)


def make_block(doc, key_values):
    vmem = pl.BlockSpec(memory_space=pltpu.VMEM)
    return pl.pallas_call(
        block_kernel,
        out_shape=jax.ShapeDtypeStruct((1, BLOCK, KV_HEADS * HEAD_DIM), jnp.bfloat16),
        in_specs=[vmem, vmem],
        out_specs=vmem,
        cost_estimate=pl.CostEstimate(flops=1000, bytes_accessed=400_000, transcendentals=0),
        name="make_block",
    )(doc, key_values)


def block_valid(y, xh, z, kind):
    across = (xh == 1) | (y >= 2)
    if kind == "own":
        return [y >= 0]
    if kind == "row":
        return [y >= 1]
    if kind == "far_row":
        return [y >= 1] * 4
    if kind == "back":
        return [y >= 2]
    if kind == "across":
        return [across]
    bit = 1 << (kind.bit_length() - 1)
    return [((z & bit) != 0) | (y >= 2), across]


COUNT = {"own": 1, "row": 1, "far_row": 4, "back": 1, "across": 1, 1: 2, 2: 2, 3: 2}


def prefill_kernel(me_ref, q_ref, own_info_ref, *refs, sources, first, last):
    blocks, rest = refs[: len(sources)], refs[len(sources) :]
    state_in = None
    if not first:
        state_in, rest = rest[0], rest[1:]
    out_ref, rest = rest[0], rest[1:]
    if last:
        state, rest = rest[0], rest[1:]
    else:
        state = out_ref.at[0]
    keys_ref, values_ref, queries_ref = rest
    step = pl.program_id(0)
    y, xh, z = me_ref[0] // 8, lax.rem(me_ref[0] // 4, 2), lax.rem(me_ref[0], 4)
    places = [(r, b) for r, source in enumerate(sources) for b in range(COUNT[source])]
    n = len(places)

    @pl.when(step == 0)
    def _():
        row = lax.broadcasted_iota(jnp.int32, (ROWS, HEAD_DIM), 0)
        lane = lax.broadcasted_iota(jnp.int32, (ROWS, HEAD_DIM), 1)

        def documents(info):
            t = info.astype(jnp.float32)[0:1, :].astype(jnp.int32)
            return sum((row >= t[:, d : d + 1]).astype(jnp.int32) for d in range(3))

        valid = []
        for source in sources:
            valid += block_valid(y, xh, z, source)
        for at, (r, b) in enumerate(places):
            doc = jnp.where(valid[at], documents(blocks[r][b, 2 * ROWS :, :]), HIDDEN_KEY)
            keys_ref[at * ROWS : (at + 1) * ROWS, HEAD_DIM:] = (lane == doc).astype(jnp.bfloat16)
        other = (lane <= HIDDEN_KEY) & (lane != documents(own_info_ref[0]))
        other = jnp.where(other, HIDDEN, 0.0).astype(jnp.bfloat16)
        for j in range(FUSED):
            queries_ref[j * ROWS : (j + 1) * ROWS, HEAD_DIM:] = other

    for at, (r, b) in enumerate(places):
        on = slice(at * ROWS, (at + 1) * ROWS)
        keys_ref[on, :HEAD_DIM] = blocks[r][b, 0:ROWS, :]
        values_ref[on, :] = blocks[r][b, ROWS : 2 * ROWS, :]
    for j in range(FUSED):
        queries_ref[j * ROWS : (j + 1) * ROWS, :HEAD_DIM] = q_ref[:, j * HEAD_DIM : (j + 1) * HEAD_DIM]

    def scores(lo, hi):
        return dot(keys_ref[lo * ROWS : hi * ROWS, :], queries_ref[...], NT)

    def own_scores():
        key = lax.broadcasted_iota(jnp.int32, (ROWS, LANES), 0)
        query = lax.rem(lax.broadcasted_iota(jnp.int32, (1, LANES), 1), ROWS)
        return jnp.where(key <= query, scores(0, 1), HIDDEN)

    def weighted(lo, hi, p):
        return dot(values_ref[lo * ROWS : hi * ROWS, :], p.astype(jnp.bfloat16), TN)

    def put(peak, total, summed):
        state[0:HEAD_DIM, :] = summed
        state[HEAD_DIM : HEAD_DIM + 8, :] = jnp.broadcast_to(peak, (8, LANES))
        state[HEAD_DIM + 8 :, :] = jnp.broadcast_to(total, (8, LANES))

    if first:
        s = own_scores()
        peak = jnp.max(s, axis=0, keepdims=True)
        p = jnp.exp2((s - peak) * TO_LOG2)
        total, summed = jnp.sum(p, axis=0, keepdims=True), weighted(0, 1, p)
    else:
        peak = state_in[0, HEAD_DIM : HEAD_DIM + 1, :]
        total = state_in[0, HEAD_DIM + 8 : HEAD_DIM + 9, :]
        summed = state_in[0, 0:HEAD_DIM, :]
    lo = 1 if first else 0
    p = jnp.exp2(scores(lo, n) * TO_LOG2 - peak * TO_LOG2)
    total = total + jnp.sum(p, axis=0, keepdims=True)
    put(peak, total, summed + weighted(lo, n, p))

    @pl.when(jnp.logical_not(jnp.max(total) < TOO_LARGE))
    def _():
        s = scores(0, n)
        if first:
            s = jnp.concatenate([own_scores(), s[ROWS:]], axis=0)
        peak = jnp.max(s, axis=0, keepdims=True)
        if not first:
            old = state_in[0, HEAD_DIM : HEAD_DIM + 1, :]
            peak = jnp.maximum(old, peak)
        p = jnp.exp2((s - peak) * TO_LOG2)
        total, summed = jnp.sum(p, axis=0, keepdims=True), weighted(0, n, p)
        if not first:
            factor = jnp.exp2((old - peak) * TO_LOG2)
            total = total + state_in[0, HEAD_DIM + 8 : HEAD_DIM + 9, :] * factor
            summed = summed + state_in[0, 0:HEAD_DIM, :] * factor
        put(peak, total, summed)

    if last:
        out = state[0:HEAD_DIM, :] / state[HEAD_DIM + 8 : HEAD_DIM + 9, :]
        out = jnp.transpose(out).astype(jnp.bfloat16)
        for j in range(FUSED):
            out_ref[:, j * HEAD_DIM : (j + 1) * HEAD_DIM] = out[j * ROWS : (j + 1) * ROWS]


def prefill_part(me, queries, own, blocks, sources, state, last, name):
    first = state is None
    n = sum(COUNT[source] for source in sources)
    steps = HEADS // FUSED
    per_kv = steps // KV_HEADS
    q_spec = pl.BlockSpec((ROWS, FUSED * HEAD_DIM), lambda i, *_: (0, i))
    state_spec = pl.BlockSpec((1, STATE, LANES), lambda i, *_: (i, 0, 0))
    in_specs = [q_spec, pl.BlockSpec((1, 16, HEAD_DIM), lambda i, *_: (0, 2 * ROWS // 16, 0))]
    in_specs += [
        pl.BlockSpec((COUNT[source], BLOCK, HEAD_DIM), lambda i, *_: (0, 0, i // per_kv)) for source in sources
    ]
    operands = [me, queries, own, *blocks]
    scratch = []
    if not first:
        in_specs.append(state_spec)
        operands.append(state)
    if last:
        out_shape = jax.ShapeDtypeStruct((ROWS, HEADS * HEAD_DIM), jnp.bfloat16)
        out_spec = q_spec
        scratch.append(pltpu.VMEM((STATE, LANES), jnp.float32))
    else:
        out_shape = jax.ShapeDtypeStruct((steps, STATE, LANES), jnp.float32)
        out_spec = state_spec
    scratch += [
        pltpu.VMEM((n * ROWS, 2 * HEAD_DIM), jnp.bfloat16),
        pltpu.VMEM((n * ROWS, HEAD_DIM), jnp.bfloat16),
        pltpu.VMEM((LANES, 2 * HEAD_DIM), jnp.bfloat16),
    ]
    return pl.pallas_call(
        functools.partial(prefill_kernel, sources=sources, first=first, last=last),
        grid_spec=pltpu.PrefetchScalarGridSpec(
            num_scalar_prefetch=1,
            grid=(steps,),
            in_specs=in_specs,
            out_specs=out_spec,
            scratch_shapes=scratch,
        ),
        out_shape=out_shape,
        compiler_params=pltpu.CompilerParams(vmem_limit_bytes=52 * 1024 * 1024),
        cost_estimate=pl.CostEstimate(
            flops=4 * n * ROWS * ROWS * HEADS * HEAD_DIM, bytes_accessed=4_000_000, transcendentals=0
        ),
        name=name,
    )(*operands)


SIDE = (2, 1, 3)


def local(prefill_queries, prefill_key_values, fill_doc, decode_queries, step_key_values, stored_key_values, cached_len):
    y, xh, z = [lax.axis_index(axis).astype(jnp.int32) for axis in CTX]
    me = (y * 2 + xh) * 4 + z

    own = make_block(fill_doc[None], prefill_key_values.reshape(2 * ROWS, KV_HEADS * HEAD_DIM))
    back1 = lax.ppermute(own, "y", [(i, i + 1) for i in range(3)])
    back2 = lax.ppermute(own, "y", [(i, i + 2) for i in range(2)])
    shares = decode_partials(cached_len, me[None], decode_queries, stored_key_values, step_key_values)

    back1, back2, shares = lax.optimization_barrier((back1, back2, shares))
    row = [back1] + [lax.ppermute(back1, "z", [(i, i ^ k) for i in range(4)]) for k in SIDE]
    across = lax.ppermute(jnp.where(xh == 0, own, back2), "xh", [(0, 1), (1, 0)])
    far_row = lax.ppermute(jnp.concatenate(row, axis=0), "xh", [(0, 1), (1, 0)])
    packs = {bit: jnp.concatenate([jnp.where((z & bit) == 0, own, back2), across], axis=0) for bit in (1, 2)}
    packs, shares = lax.optimization_barrier((packs, shares))
    side = {k: lax.ppermute(packs[min(k, 2)], "z", [(i, i ^ k) for i in range(4)]) for k in SIDE}

    shares = lax.all_to_all(shares, CTX, 0, 0)
    sources = ("own",) + ("row",) * 4 + ("back", "across")
    blocks = [own, *row, back2, across]
    state = prefill_part(me[None], prefill_queries, own, blocks, sources, None, False, "prefill_first")
    shares, state = lax.optimization_barrier((shares, state))
    spread = lax.all_to_all(join_shares(shares), CTX, 0, 0)
    sources = ("far_row",) + SIDE
    blocks = [far_row] + [side[k] for k in SIDE]
    fill_out = prefill_part(me[None], prefill_queries, own, blocks, sources, state, True, "prefill_last")
    spread, fill_out = lax.optimization_barrier((spread, fill_out))
    return fill_out, spread.transpose(1, 0, 2)


def solution(mesh):
    fine = Mesh(mesh.devices.reshape(4, 2, 4, 2, 2), ("y", "xh", "z", "xl", "c"))
    tp = ("xl", "c")
    placed = (
        P(CTX, tp),
        P(None, CTX, tp),
        P(CTX),
        P(None, None, tp),
        P(None, None, None, tp),
        P(None, None, CTX, tp),
        P(),
    )
    return jax.shard_map(
        local,
        mesh=fine,
        in_specs=placed,
        out_specs=(P(CTX, tp), P(None, None, tp)),
        check_vma=False,
    )
```

```python
import functools

import jax
import jax.numpy as jnp
from jax import lax
from jax.experimental import pallas as pl
from jax.experimental.pallas import tpu as pltpu
from jax.sharding import Mesh
from jax.sharding import PartitionSpec as P

HEAD_DIM = 128
GROUP = 8
STEPS = 4
SEQS = 32
SLOTS = 128
ROWS = 192
KV_HEADS = 2
HEADS = KV_HEADS * GROUP
PER_KV = STEPS * GROUP
PER_SEQ = STEPS * HEADS
PACKED = PER_SEQ + 16
FUSED = 8
LANES = FUSED * ROWS
BLOCK = 2 * ROWS + 16
STATE = HEAD_DIM + 16
HIDDEN = -1e30
FLOOR = -1e20
NOWHERE = -1000000
TOO_LARGE = 2.0**100
HIDDEN_KEY = 4
TO_LOG2 = HEAD_DIM**-0.5 * 1.4426950408889634
CTX = ("y", "xh", "z")
PLANE = ("xh", "z")

NT = (((1,), (1,)), ((), ()))
TN = (((0,), (0,)), ((), ()))
NN = (((1,), (0,)), ((), ()))


def dot(a, b, dims):
    return lax.dot_general(a, b, dims, preferred_element_type=jnp.float32)


def halves(value):
    high = value.astype(jnp.bfloat16).astype(jnp.float32)
    return high, (value - high).astype(jnp.bfloat16).astype(jnp.float32)


def decode_kernel(len_ref, me_ref, q_ref, kv_ref, step_ref, out_ref, rows_ref, *, per_step):
    base = pl.program_id(0) * per_step
    me = me_ref[0]
    lane = lax.broadcasted_iota(jnp.int32, (PER_SEQ, SLOTS), 1)
    tile_row = lax.broadcasted_iota(jnp.int32, (16, HEAD_DIM), 0)
    tile_lane = lax.broadcasted_iota(jnp.int32, (16, HEAD_DIM), 1)
    pick = ((tile_row == tile_lane) & (tile_row < 4)).astype(jnp.bfloat16)
    row = lax.broadcasted_iota(jnp.int32, (PER_SEQ, HEAD_DIM), 0)
    second = lax.rem(row, HEADS) >= GROUP

    for t in range(STEPS):
        for h in range(HEADS):
            at = (t * HEADS + h) * per_step
            rows_ref[at : at + per_step, :] = q_ref[t, :, h * HEAD_DIM : (h + 1) * HEAD_DIM].astype(jnp.float32)

    def queries_of(i):
        q = rows_ref[pl.ds(i, PER_SEQ, stride=per_step), :].astype(jnp.bfloat16)
        none = jnp.zeros_like(q)
        return jnp.concatenate([jnp.where(second, none, q), jnp.where(second, q, none)], axis=1)

    def scores(i):
        return jnp.where(
            lane < len_ref[base + i] - me * SLOTS, dot(queries_of(i), kv_ref[0, i], NT) * TO_LOG2, HIDDEN
        )

    def own_head(o):
        return jnp.where(second, o[:, HEAD_DIM:], o[:, :HEAD_DIM])

    def pack_stats(m_hi, m_lo, total):
        l_hi, l_lo = halves(total)
        at = lax.broadcasted_iota(jnp.int32, (total.shape[0], HEAD_DIM), 1)
        st = jnp.where(at == 0, m_hi, jnp.where(at == 1, m_lo, jnp.where(at == 2, l_hi, l_lo)))
        return dot(pick, st.astype(jnp.bfloat16), NT)

    s = jnp.concatenate([scores(i) for i in range(per_step)], axis=0)
    m_hi, m_lo = halves(jnp.maximum(jnp.max(s, axis=1, keepdims=True), FLOOR))
    p = jnp.exp2(s - (m_hi + m_lo))
    tile = pack_stats(m_hi, m_lo, jnp.sum(p, axis=1, keepdims=True))
    p = p.astype(jnp.bfloat16)
    for i in range(per_step):
        o = dot(p[i * PER_SEQ : (i + 1) * PER_SEQ], kv_ref[1, i], NN)
        out_ref[i, :PER_SEQ, :] = own_head(o).astype(jnp.bfloat16)
    for i in range(0, per_step, 2):
        pair = tile[:, i * PER_SEQ : (i + 2) * PER_SEQ]
        out_ref[i, PER_SEQ:, :] = pair.astype(jnp.bfloat16)
        swapped = jnp.concatenate([pair[:, PER_SEQ:], pair[:, :PER_SEQ]], axis=1)
        out_ref[i + 1, PER_SEQ:, :] = swapped.astype(jnp.bfloat16)

    @pl.when((me >= base) & (me < base + per_step))
    def _():
        i = me - base
        chosen = lax.broadcasted_iota(jnp.int32, (16, KV_HEADS * HEAD_DIM), 0) == lax.rem(me, 16)

        def fresh(kind):
            rows = [
                jnp.sum(jnp.where(chosen, step_ref[t, kind].astype(jnp.float32), 0.0), axis=0, keepdims=True)
                for t in range(STEPS)
            ]
            rows.append(jnp.zeros((HEAD_DIM - STEPS, KV_HEADS * HEAD_DIM), jnp.float32))
            return jnp.concatenate(rows, axis=0).astype(jnp.bfloat16)

        s = scores(i)
        f = jnp.where(lane <= row // HEADS, dot(queries_of(i), fresh(0), NT) * TO_LOG2, HIDDEN)
        m_hi, m_lo = halves(jnp.maximum(jnp.max(s, axis=1, keepdims=True), jnp.max(f, axis=1, keepdims=True)))
        p = jnp.exp2(s - (m_hi + m_lo))
        pf = jnp.exp2(f - (m_hi + m_lo))
        total = jnp.sum(p, axis=1, keepdims=True) + jnp.sum(pf, axis=1, keepdims=True)
        stats = [jnp.concatenate([x, jnp.zeros_like(x)], axis=0) for x in (m_hi, m_lo, total)]
        out_ref[i, PER_SEQ:, :] = pack_stats(*stats).astype(jnp.bfloat16)
        o = dot(p.astype(jnp.bfloat16), kv_ref[1, i], NN) + dot(pf.astype(jnp.bfloat16), fresh(1), NN)
        out_ref[i, :PER_SEQ, :] = own_head(o).astype(jnp.bfloat16)


def decode_partials(lens, me, queries, cache, fresh):
    per_step = 16
    return pl.pallas_call(
        functools.partial(decode_kernel, per_step=per_step),
        grid_spec=pltpu.PrefetchScalarGridSpec(
            num_scalar_prefetch=2,
            grid=(SEQS // per_step,),
            in_specs=[
                pl.BlockSpec((STEPS, per_step, HEADS * HEAD_DIM), lambda i, *_: (0, i, 0)),
                pl.BlockSpec((2, per_step, SLOTS, KV_HEADS * HEAD_DIM), lambda i, *_: (0, i, 0, 0)),
                pl.BlockSpec((STEPS, 2, 16, KV_HEADS * HEAD_DIM), lambda i, lens, me: (0, 0, me[0] // 16, 0)),
            ],
            out_specs=pl.BlockSpec((per_step, PACKED, HEAD_DIM), lambda i, *_: (i, 0, 0)),
            scratch_shapes=[pltpu.VMEM(((PER_SEQ + 1) * per_step, HEAD_DIM), jnp.float32)],
        ),
        out_shape=jax.ShapeDtypeStruct((SEQS, PACKED, HEAD_DIM), jnp.bfloat16),
        compiler_params=pltpu.CompilerParams(vmem_limit_bytes=62 * 1024 * 1024),
        cost_estimate=pl.CostEstimate(flops=70_000_000, bytes_accessed=5_500_000, transcendentals=262144),
        name="decode_partials",
    )(lens, me, queries, cache, fresh)


def join_kernel(in_ref, out_ref, coef, joined):
    peaks, totals = [], []
    for i in range(SEQS):
        st = in_ref[i, PER_SEQ:, :].astype(jnp.float32)
        peaks.append(st[0:1] + st[1:2])
        totals.append(st[2:3] + st[3:4])
    top = functools.reduce(jnp.maximum, peaks)
    scales = [jnp.exp2(m - top) for m in peaks]
    total = functools.reduce(jnp.add, [a * b for a, b in zip(scales, totals)])
    coef[...] = jnp.zeros_like(coef)
    for i in range(SEQS):
        coef[i : i + 1, :] = scales[i] / total
    columns = jnp.transpose(coef[...])
    acc = jnp.zeros((PER_SEQ, HEAD_DIM), jnp.float32)
    for i in range(SEQS):
        acc = acc + in_ref[i, :PER_SEQ, :].astype(jnp.float32) * columns[:PER_SEQ, i : i + 1]
    joined[:PER_SEQ, :] = acc
    heads = [joined[pl.ds(h, STEPS, stride=HEADS), :] for h in range(HEADS)]
    out = jnp.concatenate(heads, axis=1).astype(jnp.bfloat16)
    for i in range(SEQS):
        out_ref[i] = out


def join_shares(shares):
    return pl.pallas_call(
        join_kernel,
        out_shape=jax.ShapeDtypeStruct((SEQS, STEPS, HEADS * HEAD_DIM), jnp.bfloat16),
        in_specs=[pl.BlockSpec(memory_space=pltpu.VMEM)],
        out_specs=pl.BlockSpec(memory_space=pltpu.VMEM),
        scratch_shapes=[pltpu.VMEM((HEAD_DIM, HEAD_DIM), jnp.float32), pltpu.VMEM((PER_SEQ + HEADS, HEAD_DIM), jnp.float32)],
        compiler_params=pltpu.CompilerParams(vmem_limit_bytes=8 * 1024 * 1024),
        cost_estimate=pl.CostEstimate(flops=1_000_000, bytes_accessed=1_200_000, transcendentals=4096),
        name="join_shares",
    )(shares)


def block_kernel(doc_ref, kv_ref, out_ref):
    lane = lax.rem(lax.broadcasted_iota(jnp.int32, (16, KV_HEADS * HEAD_DIM), 1), HEAD_DIM)
    row = jnp.zeros((16, KV_HEADS * HEAD_DIM), jnp.float32)
    for d in range(1, 4):
        below = jnp.sum((doc_ref[...] < d).astype(jnp.float32), axis=1, keepdims=True)
        row = jnp.where(lane == d - 1, below, row)
    out_ref[0, 0 : 2 * ROWS, :] = kv_ref[...]
    out_ref[0, 2 * ROWS :, :] = row.astype(jnp.bfloat16)


def make_block(doc, key_values):
    vmem = pl.BlockSpec(memory_space=pltpu.VMEM)
    return pl.pallas_call(
        block_kernel,
        out_shape=jax.ShapeDtypeStruct((1, BLOCK, KV_HEADS * HEAD_DIM), jnp.bfloat16),
        in_specs=[vmem, vmem],
        out_specs=vmem,
        cost_estimate=pl.CostEstimate(flops=1000, bytes_accessed=400_000, transcendentals=0),
        name="make_block",
    )(doc, key_values)


def block_valid(y, xh, z, kind):
    across = (xh == 1) | (y >= 2)
    if kind == "own":
        return [y >= 0]
    if kind == "row":
        return [y >= 1]
    if kind == "far_row":
        return [y >= 1] * 4
    if kind == "back":
        return [y >= 2]
    if kind == "across":
        return [across]
    bit = 1 << (kind.bit_length() - 1)
    return [((z & bit) != 0) | (y >= 2), across]


COUNT = {"own": 1, "row": 1, "far_row": 4, "back": 1, "across": 1, 1: 2, 2: 2, 3: 2}


def prefill_kernel(me_ref, q_ref, own_info_ref, *refs, sources, first, last):
    blocks, rest = refs[: len(sources)], refs[len(sources) :]
    state_in = None
    if not first:
        state_in, rest = rest[0], rest[1:]
    out_ref, rest = rest[0], rest[1:]
    if last:
        state, rest = rest[0], rest[1:]
    else:
        state = out_ref.at[0]
    keys_ref, values_ref, queries_ref = rest
    step = pl.program_id(0)
    y, xh, z = me_ref[0] // 8, lax.rem(me_ref[0] // 4, 2), lax.rem(me_ref[0], 4)
    places = [(r, b) for r, source in enumerate(sources) for b in range(COUNT[source])]
    n = len(places)

    @pl.when(step == 0)
    def _():
        row = lax.broadcasted_iota(jnp.int32, (ROWS, HEAD_DIM), 0)
        lane = lax.broadcasted_iota(jnp.int32, (ROWS, HEAD_DIM), 1)

        def documents(info):
            t = info.astype(jnp.float32)[0:1, :].astype(jnp.int32)
            return sum((row >= t[:, d : d + 1]).astype(jnp.int32) for d in range(3))

        valid = []
        for source in sources:
            valid += block_valid(y, xh, z, source)
        for at, (r, b) in enumerate(places):
            doc = jnp.where(valid[at], documents(blocks[r][b, 2 * ROWS :, :]), HIDDEN_KEY)
            keys_ref[at * ROWS : (at + 1) * ROWS, HEAD_DIM:] = (lane == doc).astype(jnp.bfloat16)
        other = (lane <= HIDDEN_KEY) & (lane != documents(own_info_ref[0]))
        other = jnp.where(other, HIDDEN, 0.0).astype(jnp.bfloat16)
        for j in range(FUSED):
            queries_ref[j * ROWS : (j + 1) * ROWS, HEAD_DIM:] = other

    for at, (r, b) in enumerate(places):
        on = slice(at * ROWS, (at + 1) * ROWS)
        keys_ref[on, :HEAD_DIM] = blocks[r][b, 0:ROWS, :]
        values_ref[on, :] = blocks[r][b, ROWS : 2 * ROWS, :]
    for j in range(FUSED):
        queries_ref[j * ROWS : (j + 1) * ROWS, :HEAD_DIM] = q_ref[:, j * HEAD_DIM : (j + 1) * HEAD_DIM]

    def scores(lo, hi):
        return dot(keys_ref[lo * ROWS : hi * ROWS, :], queries_ref[...], NT)

    def own_scores():
        key = lax.broadcasted_iota(jnp.int32, (ROWS, LANES), 0)
        query = lax.rem(lax.broadcasted_iota(jnp.int32, (1, LANES), 1), ROWS)
        return jnp.where(key <= query, scores(0, 1), HIDDEN)

    def weighted(lo, hi, p):
        return dot(values_ref[lo * ROWS : hi * ROWS, :], p.astype(jnp.bfloat16), TN)

    def put(peak, total, summed):
        state[0:HEAD_DIM, :] = summed
        state[HEAD_DIM : HEAD_DIM + 8, :] = jnp.broadcast_to(peak, (8, LANES))
        state[HEAD_DIM + 8 :, :] = jnp.broadcast_to(total, (8, LANES))

    if first:
        s = own_scores()
        peak = jnp.max(s, axis=0, keepdims=True)
        p = jnp.exp2((s - peak) * TO_LOG2)
        total, summed = jnp.sum(p, axis=0, keepdims=True), weighted(0, 1, p)
    else:
        peak = state_in[0, HEAD_DIM : HEAD_DIM + 1, :]
        total = state_in[0, HEAD_DIM + 8 : HEAD_DIM + 9, :]
        summed = state_in[0, 0:HEAD_DIM, :]
    lo = 1 if first else 0
    p = jnp.exp2(scores(lo, n) * TO_LOG2 - peak * TO_LOG2)
    total = total + jnp.sum(p, axis=0, keepdims=True)
    put(peak, total, summed + weighted(lo, n, p))

    @pl.when(jnp.logical_not(jnp.max(total) < TOO_LARGE))
    def _():
        s = scores(0, n)
        if first:
            s = jnp.concatenate([own_scores(), s[ROWS:]], axis=0)
        peak = jnp.max(s, axis=0, keepdims=True)
        if not first:
            old = state_in[0, HEAD_DIM : HEAD_DIM + 1, :]
            peak = jnp.maximum(old, peak)
        p = jnp.exp2((s - peak) * TO_LOG2)
        total, summed = jnp.sum(p, axis=0, keepdims=True), weighted(0, n, p)
        if not first:
            factor = jnp.exp2((old - peak) * TO_LOG2)
            total = total + state_in[0, HEAD_DIM + 8 : HEAD_DIM + 9, :] * factor
            summed = summed + state_in[0, 0:HEAD_DIM, :] * factor
        put(peak, total, summed)

    if last:
        out = state[0:HEAD_DIM, :] / state[HEAD_DIM + 8 : HEAD_DIM + 9, :]
        out = jnp.transpose(out).astype(jnp.bfloat16)
        for j in range(FUSED):
            out_ref[:, j * HEAD_DIM : (j + 1) * HEAD_DIM] = out[j * ROWS : (j + 1) * ROWS]


def prefill_part(me, queries, own, blocks, sources, state, last, name):
    first = state is None
    n = sum(COUNT[source] for source in sources)
    steps = HEADS // FUSED
    per_kv = steps // KV_HEADS
    q_spec = pl.BlockSpec((ROWS, FUSED * HEAD_DIM), lambda i, *_: (0, i))
    state_spec = pl.BlockSpec((1, STATE, LANES), lambda i, *_: (i, 0, 0))
    in_specs = [q_spec, pl.BlockSpec((1, 16, HEAD_DIM), lambda i, *_: (0, 2 * ROWS // 16, 0))]
    in_specs += [
        pl.BlockSpec((COUNT[source], BLOCK, HEAD_DIM), lambda i, *_: (0, 0, i // per_kv)) for source in sources
    ]
    operands = [me, queries, own, *blocks]
    scratch = []
    if not first:
        in_specs.append(state_spec)
        operands.append(state)
    if last:
        out_shape = jax.ShapeDtypeStruct((ROWS, HEADS * HEAD_DIM), jnp.bfloat16)
        out_spec = q_spec
        scratch.append(pltpu.VMEM((STATE, LANES), jnp.float32))
    else:
        out_shape = jax.ShapeDtypeStruct((steps, STATE, LANES), jnp.float32)
        out_spec = state_spec
    scratch += [
        pltpu.VMEM((n * ROWS, 2 * HEAD_DIM), jnp.bfloat16),
        pltpu.VMEM((n * ROWS, HEAD_DIM), jnp.bfloat16),
        pltpu.VMEM((LANES, 2 * HEAD_DIM), jnp.bfloat16),
    ]
    return pl.pallas_call(
        functools.partial(prefill_kernel, sources=sources, first=first, last=last),
        grid_spec=pltpu.PrefetchScalarGridSpec(
            num_scalar_prefetch=1,
            grid=(steps,),
            in_specs=in_specs,
            out_specs=out_spec,
            scratch_shapes=scratch,
        ),
        out_shape=out_shape,
        compiler_params=pltpu.CompilerParams(vmem_limit_bytes=52 * 1024 * 1024),
        cost_estimate=pl.CostEstimate(
            flops=4 * n * ROWS * ROWS * HEADS * HEAD_DIM, bytes_accessed=4_000_000, transcendentals=0
        ),
        name=name,
    )(*operands)


SIDE = (2, 1, 3)


def local(prefill_queries, prefill_key_values, fill_doc, decode_queries, step_key_values, stored_key_values, cached_len):
    y, xh, z = [lax.axis_index(axis).astype(jnp.int32) for axis in CTX]
    me = (y * 2 + xh) * 4 + z

    own = make_block(fill_doc[None], prefill_key_values.reshape(2 * ROWS, KV_HEADS * HEAD_DIM))
    back1 = lax.ppermute(own, "y", [(i, i + 1) for i in range(3)])
    back2 = lax.ppermute(own, "y", [(i, i + 2) for i in range(2)])
    shares = decode_partials(cached_len, me[None], decode_queries, stored_key_values, step_key_values)

    back1, back2, shares = lax.optimization_barrier((back1, back2, shares))
    row = [back1] + [lax.ppermute(back1, "z", [(i, i ^ k) for i in range(4)]) for k in SIDE]
    across = lax.ppermute(jnp.where(xh == 0, own, back2), "xh", [(0, 1), (1, 0)])
    far_row = lax.ppermute(jnp.concatenate(row, axis=0), "xh", [(0, 1), (1, 0)])
    packs = {bit: jnp.concatenate([jnp.where((z & bit) == 0, own, back2), across], axis=0) for bit in (1, 2)}
    packs, shares = lax.optimization_barrier((packs, shares))
    side = {k: lax.ppermute(packs[min(k, 2)], "z", [(i, i ^ k) for i in range(4)]) for k in SIDE}

    shares = lax.all_to_all(shares, CTX, 0, 0)
    sources = ("own",) + ("row",) * 4 + ("back", "across")
    blocks = [own, *row, back2, across]
    state = prefill_part(me[None], prefill_queries, own, blocks, sources, None, False, "prefill_first")
    shares, state = lax.optimization_barrier((shares, state))
    spread = lax.all_to_all(join_shares(shares), CTX, 0, 0)
    sources = ("far_row",) + SIDE
    blocks = [far_row] + [side[k] for k in SIDE]
    fill_out = prefill_part(me[None], prefill_queries, own, blocks, sources, state, True, "prefill_last")
    spread, fill_out = lax.optimization_barrier((spread, fill_out))
    return fill_out, spread.transpose(1, 0, 2)


def solution(mesh):
    fine = Mesh(mesh.devices.reshape(4, 2, 4, 2, 2), ("y", "xh", "z", "xl", "c"))
    tp = ("xl", "c")
    placed = (
        P(CTX, tp),
        P(None, CTX, tp),
        P(CTX),
        P(None, None, tp),
        P(None, None, None, tp),
        P(None, None, CTX, tp),
        P(),
    )
    return jax.shard_map(
        local,
        mesh=fine,
        in_specs=placed,
        out_specs=(P(CTX, tp), P(None, None, tp)),
        check_vma=False,
    )
```
